32 devices in a mesh: shot: 4 (over y, core), gx: 4 (over z), gy: 2 (over x).
Axes of the slice: x: 2, y: 2, z: 4, core: 2. Of those that a mesh axis runs over, the one named last changes fastest.
Arguments:
- model_tiles: float32 [256, 64, 128], P(('shot', 'gx'), 'gy'), may hold values from 0.2 to 0.45
- owner_map: int32 [16], replicated, may hold values from 0 to 15, each once
- offsets: int32 [4], P('shot'), may hold values from 0 to 12
- field_now: float32 [4, 2, 64, 64, 128], P('shot', None, 'gx', 'gy'), may hold values from -6 to 6
- field_prev: float32 [4, 2, 64, 64, 128], P('shot', None, 'gx', 'gy'), may hold values from -6 to 6
- sources: int32 [4, 2, 3], P('shot'), may hold values from 0 to 127, as said below
- wavelet: float32 [4, 2, 8], P('shot'), may hold values from -6 to 6
- receivers: int32 [4, 256, 3], P('shot'), may hold values from 0 to 127, as said below
Outputs:
- out_now: float32 [4, 2, 64, 64, 128], P('shot', None, 'gx', 'gy')
- out_prev: float32 [4, 2, 64, 64, 128], P('shot', None, 'gx', 'gy')
- traces: float32 [4, 2, 256, 8], P('shot')
The draws below stay inside these ranges and needn't reach their ends.
Inputs may be any that keep to these rules, and one draw needn't show every extreme that they name: `sources`: each row is a cell of the group's aperture: first entry below 64, second below 64, third below 128. `receivers`: each row is a cell of the group's aperture: first entry below 64, second below 64, third below 128.
All inputs are finite; a program needn't handle non-finite values.
Results may differ from the reference program's by a relative error of at most 0.0003.
Values sent between devices are 32-bit elements; how exact they have to be, the bound alone decides.
No kernel may reach another device: no remote copies, remote signals or barrier semaphores. Data moves between devices by JAX's collectives and lax.ppermute only.
A program may use at most 128 MiB of HBM per device.

```python
import jax
import jax.numpy as jnp
from jax import lax

BX = 16
BZ = 128
SHOTS = 2
STEPS = 8
RECS = 256
GROUPS = 4
TCOLS = 16
NXA = 64
NYA = 64
N_GX = 4


def cell_points(key, amount):
    key_x, key_y, key_z = jax.random.split(key, 3)
    along_x = jax.random.randint(key_x, (GROUPS, amount), 0, NXA, dtype=jnp.int32)
    along_y = jax.random.randint(key_y, (GROUPS, amount), 0, NYA, dtype=jnp.int32)
    along_z = jax.random.randint(key_z, (GROUPS, amount), 0, BZ, dtype=jnp.int32)
    points = jnp.stack([along_x, along_y, along_z], axis=-1)
    points = points.at[0, 0].set(jnp.array([NXA - 1, NYA - 1, BZ - 1], dtype=jnp.int32))
    points = points.at[0, amount - 1].set(jnp.zeros((3,), jnp.int32))
    return points


def draw_sources(key, part):
    return cell_points(jax.random.fold_in(key, 11), SHOTS)


def draw_receivers(key, part):
    return cell_points(jax.random.fold_in(key, 23), RECS)


def place_ends(drawn, stream_key, least, largest):
    extent = drawn.shape
    spot = [jax.random.randint(jax.random.fold_in(stream_key, axis), (), 0, extent[axis]) for axis in range(len(extent))]
    drawn = drawn.at[tuple(spot)].set(least)
    longest = extent.index(max(extent))
    spot[longest] = (spot[longest] + 1) % extent[longest]
    return drawn.at[tuple(spot)].set(largest)


def levels(rng, dims, cuts, least, high):
    loudness, own = 1.0, jax.random.fold_in(rng, 6)
    for dim, parts in cuts:
        steps = jnp.exp(jax.random.uniform(jax.random.fold_in(own, dim), (parts,), jnp.float32, least / len(cuts), high / len(cuts)))
        loudness = loudness * jnp.repeat(steps, dims[dim] // parts).reshape([-1 if axis == dim else 1 for axis in range(len(dims))])
    return loudness


def scatter_about(rng, extent, scale, most, shards=(), held_as=jnp.bfloat16):
    result = scale * jax.random.normal(rng, extent, jnp.float32)
    if shards:
        result = result * levels(rng, extent, shards, -0.22, 0.18)
    return jnp.clip(result, -most, most).astype(held_as)


def setup_inputs(seed: int = 0) -> dict:
    keys = jax.random.split(jax.random.key(seed), 9)
    model_tiles = jnp.clip(0.2 + 0.24999999 * jax.random.uniform(keys[0], (TCOLS * BX, NYA, BZ), jnp.float32) ** levels(keys[0], (TCOLS * BX, NYA, BZ), ((0, 16), (1, 2)), -0.2, 0.2), 0.2, 0.45)
    owner_map = jax.random.permutation(keys[1], TCOLS).astype(jnp.int32)
    offsets = place_ends(jax.random.randint(keys[2], (GROUPS,), 0, TCOLS - N_GX + 1), jax.random.fold_in(keys[2], 1), 0, TCOLS - N_GX).astype(jnp.int32)
    field_now = scatter_about(keys[3], (GROUPS, SHOTS, NXA, NYA, BZ), 1.0, 6.0, ((0, 4), (2, 4), (3, 2)), jnp.float32)
    field_prev = scatter_about(keys[4], (GROUPS, SHOTS, NXA, NYA, BZ), 1.0, 6.0, ((0, 4), (2, 4), (3, 2)), jnp.float32)
    sources = draw_sources(jax.random.fold_in(keys[8], 71), 0)
    wavelet = scatter_about(keys[6], (GROUPS, SHOTS, STEPS), 1.0, 6.0, ((0, 4),), jnp.float32)
    receivers = draw_receivers(jax.random.fold_in(keys[8], 71), 0)
    return {"model_tiles": model_tiles, "owner_map": owner_map, "offsets": offsets, "field_now": field_now, "field_prev": field_prev, "sources": sources, "wavelet": wavelet, "receivers": receivers}


center_weight = -2.5
near_weight = 4.0 / 3.0
far_weight = -1.0 / 12.0
damp_peak = 0.3


def laplace(padded):
    middle = padded[:, 2:-2, 2:-2, 2:-2]
    along_x = center_weight * middle + near_weight * (padded[:, 3:-1, 2:-2, 2:-2] + padded[:, 1:-3, 2:-2, 2:-2]) + far_weight * (padded[:, 4:, 2:-2, 2:-2] + padded[:, :-4, 2:-2, 2:-2])
    along_y = center_weight * middle + near_weight * (padded[:, 2:-2, 3:-1, 2:-2] + padded[:, 2:-2, 1:-3, 2:-2]) + far_weight * (padded[:, 2:-2, 4:, 2:-2] + padded[:, 2:-2, :-4, 2:-2])
    along_z = center_weight * middle + near_weight * (padded[:, 2:-2, 2:-2, 3:-1] + padded[:, 2:-2, 2:-2, 1:-3]) + far_weight * (padded[:, 2:-2, 2:-2, 4:] + padded[:, 2:-2, 2:-2, :-4])
    return along_x + along_y + along_z


def damping(x_cells, y_cells, width, x_total, y_total):
    x_depth = jnp.maximum(width - jnp.minimum(x_cells + 1, x_total - x_cells), 0).astype(jnp.float32) / width
    y_depth = jnp.maximum(width - jnp.minimum(y_cells + 1, y_total - y_cells), 0).astype(jnp.float32) / width
    return damp_peak * (x_depth[:, None] * x_depth[:, None] + y_depth[None, :] * y_depth[None, :])


def injection(x_cells, y_cells, z_cells, source_cells, amplitude):
    on_x = (x_cells[None, :] == source_cells[:, 0:1]).astype(jnp.float32)
    on_y = (y_cells[None, :] == source_cells[:, 1:2]).astype(jnp.float32)
    on_z = (z_cells[None, :] == source_cells[:, 2:3]).astype(jnp.float32)
    return amplitude[:, None, None, None] * on_x[:, :, None, None] * on_y[:, None, :, None] * on_z[:, None, None, :]


def advance(padded, previous, coef, damp, inject):
    middle = padded[:, 2:-2, 2:-2, 2:-2]
    return (2.0 * middle - (1.0 - damp) * previous + coef * laplace(padded) + inject) / (1.0 + damp)


def reference(model_tiles, owner_map, offsets, field_now, field_prev, sources, wavelet, receivers):
    blocks = model_tiles.reshape(TCOLS, BX, NYA, BZ)
    model = jnp.take(blocks, owner_map.astype(jnp.int32), axis=0).reshape(TCOLS * BX, NYA, BZ)
    x_cells = jnp.arange(NXA, dtype=jnp.int32)
    y_cells = jnp.arange(NYA, dtype=jnp.int32)
    z_cells = jnp.arange(BZ, dtype=jnp.int32)
    damp = damping(x_cells, y_cells, BX, NXA, NYA)[:, :, None]
    now_list = []
    prev_list = []
    trace_list = []
    for group in range(GROUPS):
        speed = lax.dynamic_slice_in_dim(model, (offsets[group] * BX).astype(jnp.int32), NXA, 0)
        coef = speed * speed
        current = field_now[group]
        previous = field_prev[group]
        samples = []
        for step in range(STEPS):
            padded = jnp.pad(current, ((0, 0), (2, 2), (2, 2), (2, 2)))
            inject = injection(x_cells, y_cells, z_cells, sources[group], wavelet[group, :, step])
            fresh = advance(padded, previous, coef, damp, inject)
            samples.append(fresh[:, receivers[group, :, 0], receivers[group, :, 1], receivers[group, :, 2]])
            previous = current
            current = fresh
        now_list.append(current)
        prev_list.append(previous)
        trace_list.append(jnp.stack(samples, axis=-1))
    return jnp.stack(now_list), jnp.stack(prev_list), jnp.stack(trace_list)
```

```python
import functools

import jax
import jax.numpy as jnp
from jax import lax
from jax.experimental import pallas as pl
from jax.experimental.pallas import tpu as pltpu
from jax.sharding import Mesh
from jax.sharding import PartitionSpec as P

STEPS = 8
HALO = 2 * STEPS
PAD = 8

near_weight = 4.0 / 3.0
centre_ratio = 7.5 * 3.0 / 4.0
far_ratio = 1.0 / 16.0
damp_peak = 0.3

SMEM = pl.BlockSpec(memory_space=pltpu.SMEM)
ANY = pl.BlockSpec(memory_space=pl.ANY)
VMEM = pl.BlockSpec(memory_space=pltpu.VMEM)


def pairs(count, parity):
    return [
        pair
        for i in range(parity, count - 1, 2)
        for pair in ((i, i + 1), (i + 1, i))
    ]


def joint(first, second, count):
    return [(a * count + b, c * count + d) for a, c in first for b, d in second]


def pick_kernel(columns, where, stored, other, out, sems):
    targets = out.shape[0]
    across = where[1]
    core = where[0]
    copies = []
    for t in range(targets):
        block = columns[t]
        owner_core = (block // across) % 2
        row = (block // (2 * across)) * across + block % across
        here = pltpu.make_async_copy(stored.at[row], out.at[t], sems.at[t])
        there = pltpu.make_async_copy(other.at[row], out.at[t], sems.at[t])
        pl.when(owner_core == core)(here.start)
        pl.when(owner_core != core)(there.start)
        copies.append(here)
    for copy in copies:
        copy.wait()


def pick(columns, where, stored, other):
    targets = stored.shape[0]
    return pl.pallas_call(
        pick_kernel,
        out_shape=jax.ShapeDtypeStruct(stored.shape, stored.dtype),
        in_specs=[SMEM, SMEM, ANY, ANY],
        out_specs=ANY,
        scratch_shapes=[pltpu.SemaphoreType.DMA((targets,))],
        name="pick_slices",
    )(columns, where, stored, other)


def list_kernel(block_x, block_y, starts, receivers, out):
    total = receivers.shape[0] // 3

    def body(r, count):
        x = receivers[3 * r] - starts[0]
        y = receivers[3 * r + 1] - starts[1]
        inside = (x >= 0) & (x < block_x) & (y >= 0) & (y < block_y)
        out[1 + 2 * count] = r
        out[2 + 2 * count] = x * block_y + y
        return count + inside.astype(jnp.int32)

    out[0] = lax.fori_loop(0, total, body, jnp.int32(0))


def list_receivers(block_x, block_y, starts, receivers):
    total = receivers.shape[0]
    return pl.pallas_call(
        functools.partial(list_kernel, block_x, block_y),
        out_shape=jax.ShapeDtypeStruct((2 * total + 8,), jnp.int32),
        in_specs=[SMEM, SMEM],
        out_specs=SMEM,
        name="list_receivers",
    )(starts, receivers.reshape(-1))


def window_kernel(
    sizes,
    starts,
    sources,
    amplitudes,
    local_list,
    lanes,
    now,
    prev,
    now_x,
    prev_x,
    sides,
    corners,
    speed,
    speed_x,
    speed_y,
    speed_xy,
    out_now,
    out_prev,
    partial,
    now_ext,
    prev_ext,
    near,
    twice,
    samples,
    sems,
    out_sems,
):
    block_x, block_y, total_x, total_y, ny = sizes
    rows = now_ext.shape[2]
    planes = now_ext.shape[1]
    shots = now_ext.shape[0]
    column, row = starts[0], starts[1]
    odd_x, odd_y = column % 2, row % 2
    own = pl.multiple_of(PAD + (HALO * odd_y if ny == 2 else HALO), 8)
    high_x = [odd_x == 0, odd_x == 1]
    high_y = [odd_y == 0, odd_y == 1]
    x_at = [jnp.where(h, HALO + block_x, 0) for h in high_x]
    y_at = [
        pl.multiple_of(jnp.where(h, own + block_y, own - HALO), 8) for h in high_y
    ]
    near_x = [jnp.where(h, 0, HALO // 2) for h in high_x]
    near_y = [
        pl.multiple_of(jnp.where(h, own + block_y, own - HALO // 2), 8) for h in high_y
    ]
    far_y = [
        pl.multiple_of(jnp.where(h, own + block_y + HALO // 2, own - HALO), 8)
        for h in high_y
    ]
    half = HALO // 2
    copies = []

    def fetch(src, dst):
        copy = pltpu.make_async_copy(src, dst, sems.at[len(copies)])
        copy.start()
        copies.append(copy)

    y_count = speed_y.shape[0]
    own_rows = pl.ds(own, block_y)
    fetch(now, now_ext.at[:, pl.ds(HALO, block_x), own_rows])
    fetch(prev, prev_ext.at[:, pl.ds(HALO, block_x), own_rows])
    for e in range(2):
        at = pl.ds(x_at[e], block_x)
        fetch(now_x[e], now_ext.at[:, at, own_rows])
        fetch(prev_x[e], prev_ext.at[:, at, own_rows])
    for f in range(y_count):
        at = pl.ds(y_at[f], HALO)
        fetch(sides.at[f, 0], now_ext.at[:, pl.ds(HALO, block_x), at])
        fetch(sides.at[f, 1], prev_ext.at[:, pl.ds(HALO, block_x), at])
        for e in range(2):
            at_near = pl.ds(x_at[e] + near_x[e], half)
            at_far = pl.ds(x_at[e] + half - near_x[e], half)
            for k, ext in enumerate((now_ext, prev_ext)):
                fetch(
                    corners.at[f, e, k, :, :, pl.ds(0, HALO)],
                    ext.at[:, at_near, at],
                )
                fetch(
                    corners.at[f, e, k, :, :, pl.ds(HALO, half)],
                    ext.at[:, at_far, pl.ds(near_y[f], half)],
                )
    field_copies = len(copies)
    fetch(speed, near.at[pl.ds(HALO, block_x), own_rows])
    for e in range(2):
        fetch(speed_x[e], near.at[pl.ds(x_at[e], block_x), own_rows])
    for f in range(y_count):
        at = pl.ds(y_at[f], HALO)
        fetch(speed_y.at[f], near.at[pl.ds(HALO, block_x), at])
        for e in range(2):
            fetch(speed_xy.at[f, e], near.at[pl.ds(x_at[e], block_x), at])

    blank = jnp.zeros((PAD, now_ext.shape[3]), jnp.float32)
    for ext in (now_ext, prev_ext):
        for s in range(shots):

            def clear(x, _):
                ext[s, x, pl.ds(0, PAD)] = blank
                ext[s, x, pl.ds(rows - PAD, PAD)] = blank
                return 0

            lax.fori_loop(0, planes, clear, 0)
            for f in range(y_count):
                for e in range(2):

                    def clear_far(x, _):
                        ext[s, x_at[e] + half - near_x[e] + x, pl.ds(far_y[f], half)] = blank
                        return 0

                    lax.fori_loop(0, half, clear_far, 0)

    def depth_in(cell, total):
        inside = (cell >= 0) & (cell < total)
        depth = jnp.maximum(
            block_x - jnp.minimum(cell + 1, total - cell), 0
        ).astype(jnp.float32) / block_x
        return inside, depth

    x_first = column * block_x - HALO
    y_first = row * block_y - own
    shape = (rows, now_ext.shape[3])
    y_in, y_depth = depth_in(lax.broadcasted_iota(jnp.int32, shape, 0) + y_first, total_y)
    y_part = y_depth * y_depth

    for copy in copies:
        copy.wait()

    def prepare(x, _):
        x_in, x_depth = depth_in(jnp.full(shape, x + x_first, jnp.int32), total_x)
        inverse = 1.0 / (1.0 + damp_peak * (x_depth * x_depth + y_part))
        inverse = jnp.where(x_in & y_in, inverse, 0.0)
        v = near[x]
        near[x] = jnp.where(x_in & y_in, inverse * (v * v) * near_weight, 0.0)
        twice[x] = 2.0 * inverse
        return 0

    lax.fori_loop(2, planes - 2, prepare, 0)

    depth = now_ext.shape[3]
    lane = lax.broadcasted_iota(jnp.int32, (8, depth), 1)
    ahead_1, ahead_2 = lane < depth - 1, lane < depth - 2
    behind_1, behind_2 = lane >= 1, lane >= 2
    lane_row = lax.broadcasted_iota(jnp.int32, (1, depth), 1)

    cur, old = now_ext, prev_ext
    for step in range(1, STEPS + 1):
        reach = 2 * (STEPS - step)
        side = -(-reach // 8)
        if ny == 2:
            first = pl.multiple_of(own - 8 * side * odd_y, 8)
            tiles = block_y // 8 + side
        else:
            first = pl.multiple_of(own - 8 * side, 8)
            tiles = block_y // 8 + 2 * side

        def plane(x, _, cur=cur, old=old, first=first, tiles=tiles):
            for j in range(tiles):
                base = first + 8 * j
                at = pl.ds(pl.multiple_of(base, 8), 8)
                n, a = near[x, at], twice[x, at]
                for s in range(shots):
                    c = cur[s, x, at]
                    close = cur[s, x - 1, at] + cur[s, x + 1, at]
                    wide = cur[s, x - 2, at] + cur[s, x + 2, at]
                    close += cur[s, x, pl.ds(base - 1, 8)] + cur[s, x, pl.ds(base + 1, 8)]
                    wide += cur[s, x, pl.ds(base - 2, 8)] + cur[s, x, pl.ds(base + 2, 8)]
                    close += jnp.where(ahead_1, pltpu.roll(c, depth - 1, 1), 0.0)
                    close += jnp.where(behind_1, pltpu.roll(c, 1, 1), 0.0)
                    wide += jnp.where(ahead_2, pltpu.roll(c, depth - 2, 1), 0.0)
                    wide += jnp.where(behind_2, pltpu.roll(c, 2, 1), 0.0)
                    p = old[s, x, at]
                    lap = close - far_ratio * wide - centre_ratio * c
                    old[s, x, at] = p + a * (c - p) + n * lap
            return 0

        lax.fori_loop(2 * step, planes - 2 * step, plane, 0)

        for s in range(shots):
            sx = sources[3 * s] - x_first
            sy = sources[3 * s + 1] - y_first
            sz = sources[3 * s + 2]
            amplitude = amplitudes[s * STEPS + step - 1]
            inside = (
                (sx >= 2 * step)
                & (sx < planes - 2 * step)
                & (sy >= first)
                & (sy < first + 8 * tiles)
            )

            @pl.when(inside)
            def _(old=old, s=s, sx=sx, sy=sy, sz=sz, amplitude=amplitude):
                at = pl.ds(sy, 1)
                old[s, sx, at] += jnp.where(lane_row == sz, amplitude, 0.0)

        cur, old = old, cur

        def take(k, _, cur=cur, step=step):
            r = local_list[1 + 2 * k]
            cell = local_list[2 + 2 * k]
            x = HALO + cell // block_y
            y = own + cell % block_y
            for s in range(shots):
                samples[s * STEPS + step - 1, pl.ds(r, 1)] = cur[s, x, pl.ds(y, 1)]
            return 0

        lax.fori_loop(0, local_list[0], take, 0)
        if step >= STEPS - 1:
            out = out_prev if step == STEPS - 1 else out_now
            copy = pltpu.make_async_copy(
                cur.at[:, pl.ds(HALO, block_x), own_rows],
                out,
                out_sems.at[step - STEPS + 1],
            )
            copy.start()
            if step == STEPS - 1:
                first_out = copy
            else:
                last_out = copy

    total = lanes.shape[0]
    mask = lanes[...] == lax.broadcasted_iota(jnp.int32, (total, depth), 1)
    for k in range(shots * STEPS):
        taken = jnp.where(mask, samples[k], 0.0)
        values = jnp.sum(taken, axis=1)
        for copy_to in range(partial.shape[0]):
            partial[copy_to, k] = values
    first_out.wait()
    last_out.wait()


def window(sizes, starts, sources, amplitudes, local_list, lanes, now, prev, now_x, prev_x, sides, corners, speed, speed_x, speed_y, speed_xy, copies):
    block_x, block_y, total_x, total_y, ny = sizes
    shots, _, _, depth = now.shape
    planes = block_x + 2 * HALO
    rows = block_y + (HALO if ny == 2 else 2 * HALO) + 2 * PAD
    recs = lanes.shape[0]

    def kernel(starts, sources, amplitudes, local_list, lanes, now, prev, n0, n1, p0, p1, sides, corners, speed, v0, v1, *rest):
        window_kernel(
            sizes, starts, sources, amplitudes, local_list, lanes, now, prev,
            (n0, n1), (p0, p1), sides, corners, speed, (v0, v1), *rest,
        )

    return pl.pallas_call(
        kernel,
        out_shape=(
            jax.ShapeDtypeStruct(now.shape, now.dtype),
            jax.ShapeDtypeStruct(now.shape, now.dtype),
            jax.ShapeDtypeStruct((copies, shots * STEPS, recs), now.dtype),
        ),
        in_specs=[SMEM, SMEM, SMEM, SMEM, VMEM] + [ANY] * 13,
        out_specs=(ANY, ANY, VMEM),
        scratch_shapes=[
            pltpu.VMEM((shots, planes, rows, depth), jnp.float32),
            pltpu.VMEM((shots, planes, rows, depth), jnp.float32),
            pltpu.VMEM((planes, rows, depth), jnp.float32),
            pltpu.VMEM((planes, rows, depth), jnp.float32),
            pltpu.VMEM((shots * STEPS, recs, depth), jnp.float32),
            pltpu.SemaphoreType.DMA((48,)),
            pltpu.SemaphoreType.DMA((2,)),
        ],
        compiler_params=pltpu.CompilerParams(vmem_limit_bytes=40 * 2**20),
        name="wave_window",
    )(
        starts, sources, amplitudes, local_list, lanes, now, prev, *now_x, *prev_x,
        sides, corners, speed, *speed_x, speed_y, speed_xy,
    )


def local(model_tiles, owner_map, offsets, field_now, field_prev, sources, wavelet, receivers):
    block_x, block_y, depth = model_tiles.shape
    nx, ny, groups = lax.axis_size("gx"), lax.axis_size("gy"), lax.axis_size("sy")
    column, row, core = lax.axis_index("gx"), lax.axis_index("gy"), lax.axis_index("core")
    shot_row = lax.axis_index("sy")
    total_x, total_y = block_x * nx, block_y * ny
    now, prev = field_now[0], field_prev[0]
    x_perms = [pairs(nx, 0), pairs(nx, 1)]
    y_perms = [pairs(ny, f) for f in range(2 if ny > 2 else 1)]
    odd_x, odd_y = column % 2, row % 2
    low_rows, high_rows = 0, block_y - HALO
    half = HALO // 2

    spread = lax.all_to_all(model_tiles, ("sy", "gx"), 0, 0, tiled=True)
    other = lax.ppermute(spread, "core", [(0, 1), (1, 0)])

    now_x = [lax.ppermute(now, "gx", perm) for perm in x_perms]
    prev_x = [lax.ppermute(prev, "gx", perm) for perm in x_perms]

    def sent_rows(f):
        return jnp.where(odd_y == f, high_rows, low_rows)

    def near_planes(e):
        return jnp.where(odd_x == e, 0, half)

    sides, corners = [], []
    for f, perm in enumerate(y_perms):
        start = sent_rows(f)
        cut = jnp.stack(
            [lax.dynamic_slice_in_dim(v, start, HALO, axis=2) for v in (now, prev)]
        )
        sides.append(lax.ppermute(cut, "gy", perm))
        near_start = jnp.where(odd_y == f, block_y - half, 0)
        cut = []
        for e in range(2):
            for v in (now_x[e], prev_x[e]):
                close = lax.dynamic_slice_in_dim(v, near_planes(e), half, axis=1)
                close = lax.dynamic_slice_in_dim(close, start, HALO, axis=2)
                wide = lax.dynamic_slice_in_dim(v, half - near_planes(e), half, axis=1)
                wide = lax.dynamic_slice_in_dim(wide, near_start, half, axis=2)
                cut.append(jnp.concatenate([close, wide], axis=2))
        cut = jnp.stack(cut).reshape((2, 2) + cut[0].shape)
        corners.append(lax.ppermute(cut, "gy", perm))
    sides, corners = jnp.stack(sides), jnp.stack(corners)

    shifts = jnp.zeros((groups,), jnp.int32)
    for turn in range(groups):
        came = offsets if turn == 0 else lax.ppermute(
            offsets, "sy", [(i, (i + turn) % groups) for i in range(groups)]
        )
        at = (shot_row - turn) % groups
        shifts = jnp.where(jnp.arange(groups) == at, came, shifts)
    columns = (shifts[:, None] + jnp.arange(nx, dtype=jnp.int32)[None, :]).reshape(-1)
    stored_in = jnp.sum(
        jnp.where(
            columns[:, None] == jnp.arange(owner_map.shape[0], dtype=jnp.int32)[None, :],
            owner_map[None, :],
            0,
        ),
        axis=1,
    )
    targets = groups * nx
    slice_shape = (targets, block_x // targets, block_y, depth)
    picked = pick(
        stored_in,
        jnp.stack([core, jnp.int32(nx)]),
        spread.reshape(slice_shape),
        other.reshape(slice_shape),
    )
    speed = lax.all_to_all(picked.reshape(model_tiles.shape), ("sy", "gx"), 0, 0, tiled=True)
    speed_x = [lax.ppermute(speed, "gx", perm) for perm in x_perms]
    speed_y, speed_xy = [], []
    for f, perm in enumerate(y_perms):
        cut = lax.dynamic_slice_in_dim(speed, sent_rows(f), HALO, axis=1)
        speed_y.append(lax.ppermute(cut, "gy", perm))
        speed_xy.append(
            jnp.stack([lax.ppermute(cut, ("gx", "gy"), joint(x_perm, perm, ny)) for x_perm in x_perms])
        )

    starts = jnp.stack([column, row]).astype(jnp.int32)
    cells = receivers[0]
    local_list = list_receivers(
        block_x, block_y, starts * jnp.array([block_x, block_y], jnp.int32), cells
    )
    local_x, local_y = cells[:, 0] - column * block_x, cells[:, 1] - row * block_y
    inside = (local_x >= 0) & (local_x < block_x) & (local_y >= 0) & (local_y < block_y)
    lanes = jnp.broadcast_to(jnp.where(inside, cells[:, 2], -1)[:, None], (cells.shape[0], depth))
    place = sources[0]
    x_depth = jnp.maximum(block_x - jnp.minimum(place[:, 0] + 1, total_x - place[:, 0]), 0).astype(jnp.float32) / block_x
    y_depth = jnp.maximum(block_x - jnp.minimum(place[:, 1] + 1, total_y - place[:, 1]), 0).astype(jnp.float32) / block_x
    damp = damp_peak * (x_depth * x_depth + y_depth * y_depth)
    amplitudes = wavelet[0] / (1.0 + damp)[:, None]

    out_now, out_prev, partial = window(
        (block_x, block_y, total_x, total_y, ny),
        starts, place.reshape(-1), amplitudes.reshape(-1), local_list, lanes,
        now, prev, now_x, prev_x, sides, corners,
        speed, speed_x, jnp.stack(speed_y), jnp.stack(speed_xy), nx * ny,
    )
    gathered = lax.all_to_all(partial, ("gx", "gy"), 0, 0, tiled=True)
    shots = now.shape[0]
    traces = jnp.sum(gathered, axis=0).reshape(shots, STEPS, -1).transpose(0, 2, 1)
    return (out_now[None], out_prev[None], traces[None])


def solution(mesh):
    shape = dict(zip(mesh.axis_names, mesh.devices.shape))
    cores = 2 if shape["shot"] % 2 == 0 else 1
    fine = Mesh(
        mesh.devices.reshape(shape["shot"] // cores, cores, shape["gx"], shape["gy"]),
        ("sy", "core", "gx", "gy"),
    )
    shot = ("sy", "core")
    field = P(shot, None, "gx", "gy", None)
    return jax.shard_map(
        local,
        mesh=fine,
        in_specs=(
            P(("sy", "core", "gx"), "gy", None),
            P(),
            P(shot),
            field,
            field,
            P(shot, None, None),
            P(shot, None, None),
            P(shot, None, None),
        ),
        out_specs=(field, field, P(shot, None, None, None)),
        check_vma=False,
    )
```

```python
import functools

import jax
import jax.numpy as jnp
from jax import lax
from jax.experimental import pallas as pl
from jax.experimental.pallas import tpu as pltpu
from jax.sharding import Mesh
from jax.sharding import PartitionSpec as P

STEPS = 8
HALO = 2 * STEPS
PAD = 8
GROUP = 4
BATCH = 4

near_weight = 4.0 / 3.0
centre_part = -7.5 * 0.75
far_part = -1.0 / 16.0
damp_peak = 0.3

SMEM = pl.BlockSpec(memory_space=pltpu.SMEM)
ANY = pl.BlockSpec(memory_space=pl.ANY)
VMEM = pl.BlockSpec(memory_space=pltpu.VMEM)


def pairs(count, parity):
    return [
        pair
        for i in range(parity, count - 1, 2)
        for pair in ((i, i + 1), (i + 1, i))
    ]


def joint(first, second, count):
    return [(a * count + b, c * count + d) for a, c in first for b, d in second]


def prepare_kernel(block_x, block_y, places, owner_map, shifts, receivers, stored_in, local_list):
    column, row, across = places[0], places[1], places[2]
    targets = stored_in.shape[0]
    for t in range(targets):
        stored_in[t] = owner_map[shifts[t]]
    x_first, y_first = column * block_x, row * block_y
    total = receivers.shape[1]
    batch = 8

    def body(g, count):
        for i in range(batch):
            r = g * batch + i
            x = receivers[0, r] - x_first
            y = receivers[1, r] - y_first
            inside = (x >= 0) & (x < block_x) & (y >= 0) & (y < block_y)
            local_list[1 + 3 * count] = r
            local_list[2 + 3 * count] = x * block_y + y
            local_list[3 + 3 * count] = receivers[2, r]
            count = count + inside.astype(jnp.int32)
        return count

    count = lax.fori_loop(0, total // batch, body, jnp.int32(0))
    local_list[0] = count
    for i in range(BATCH):
        local_list[1 + 3 * (count + i)] = total
        local_list[2 + 3 * (count + i)] = 0
        local_list[3 + 3 * (count + i)] = 0


def prepare(block_x, block_y, places, owner_map, shifts, receivers):
    total = receivers.shape[1]
    return pl.pallas_call(
        functools.partial(prepare_kernel, block_x, block_y),
        out_shape=(
            jax.ShapeDtypeStruct(shifts.shape, jnp.int32),
            jax.ShapeDtypeStruct((3 * (total + BATCH) + 8,), jnp.int32),
        ),
        in_specs=[SMEM] * 4,
        out_specs=(SMEM, SMEM),
        name="prepare_lists",
    )(places, owner_map, shifts, receivers)


def pick_kernel(stored_in, places, stored, other, out, sems):
    targets = out.shape[0]
    across, core = places[2], places[3]
    copies = []
    for t in range(targets):
        block = stored_in[t]
        owner_core = (block // across) % 2
        row = (block // (2 * across)) * across + block % across
        here = pltpu.make_async_copy(stored.at[row], out.at[t], sems.at[t])
        there = pltpu.make_async_copy(other.at[row], out.at[t], sems.at[t])
        pl.when(owner_core == core)(here.start)
        pl.when(owner_core != core)(there.start)
        copies.append(here)
    for copy in copies:
        copy.wait()


def pick(stored_in, places, stored, other):
    targets = stored.shape[0]
    return pl.pallas_call(
        pick_kernel,
        out_shape=jax.ShapeDtypeStruct(stored.shape, stored.dtype),
        in_specs=[SMEM, SMEM, ANY, ANY],
        out_specs=VMEM,
        scratch_shapes=[pltpu.SemaphoreType.DMA((targets,))],
        name="pick_slices",
    )(stored_in, places, stored, other)


def corner_kernel(block_y, parity_y, places, first, second, out, sems):
    half = HALO // 2
    odd_x, odd_y = places[0] % 2, places[1] % 2
    above = odd_y == parity_y
    start = pl.multiple_of(jnp.where(above, block_y - HALO, 0), 8)
    near_start = pl.multiple_of(jnp.where(above, block_y - half, 0), 8)
    copies = []
    for e, block in enumerate((first, second)):
        near = jnp.where(odd_x == e, 0, half)
        copies.append(
            pltpu.make_async_copy(
                block.at[:, pl.ds(near, half), pl.ds(start, HALO)],
                out.at[e, :, :, pl.ds(0, HALO)],
                sems.at[2 * e],
            )
        )
        copies.append(
            pltpu.make_async_copy(
                block.at[:, pl.ds(half - near, half), pl.ds(near_start, half)],
                out.at[e, :, :, pl.ds(HALO, half)],
                sems.at[2 * e + 1],
            )
        )
    for copy in copies:
        copy.start()
    for copy in copies:
        copy.wait()


def pack_corners(parity_y, places, blocks):
    shots, _, block_y, depth = blocks[0].shape
    half = HALO // 2
    return pl.pallas_call(
        functools.partial(corner_kernel, block_y, parity_y),
        out_shape=jax.ShapeDtypeStruct((2, shots, half, HALO + half, depth), jnp.float32),
        in_specs=[SMEM, ANY, ANY],
        out_specs=VMEM,
        scratch_shapes=[pltpu.SemaphoreType.DMA((4,))],
        name="pack_corners",
    )(places, *blocks)


def side_kernel(block_y, parity_y, places, now, prev, out, sems):
    start = pl.multiple_of(jnp.where(places[1] % 2 == parity_y, block_y - HALO, 0), 8)
    copies = [
        pltpu.make_async_copy(block.at[:, :, pl.ds(start, HALO)], out.at[k], sems.at[k])
        for k, block in enumerate((now, prev))
    ]
    for copy in copies:
        copy.start()
    for copy in copies:
        copy.wait()


def pack_sides(parity_y, places, now, prev):
    shots, block_x, block_y, depth = now.shape
    return pl.pallas_call(
        functools.partial(side_kernel, block_y, parity_y),
        out_shape=jax.ShapeDtypeStruct((2, shots, block_x, HALO, depth), jnp.float32),
        in_specs=[SMEM, ANY, ANY],
        out_specs=VMEM,
        scratch_shapes=[pltpu.SemaphoreType.DMA((2,))],
        name="pack_sides",
    )(places, now, prev)


def window_kernel(
    sizes,
    starts,
    sources,
    amplitudes,
    local_list,
    now,
    prev,
    now_x,
    prev_x,
    sides,
    corners_now,
    corners_prev,
    speed,
    speed_x,
    speed_y,
    speed_xy,
    out_now,
    out_prev,
    partial,
    ext_all,
    samples,
    sems,
    out_sems,
):
    block_x, block_y, total_x, total_y, ny = sizes
    half_way = (ext_all.shape[0] - 2) // 2
    now_ext, prev_ext = ext_all.at[pl.ds(0, half_way)], ext_all.at[pl.ds(half_way, half_way)]
    near, twice = ext_all.at[2 * half_way], ext_all.at[2 * half_way + 1]
    rows = now_ext.shape[2]
    planes = now_ext.shape[1]
    shots = now_ext.shape[0]
    column, row = starts[0], starts[1]
    odd_x, odd_y = column % 2, row % 2
    own = pl.multiple_of(PAD + (HALO * odd_y if ny == 2 else HALO), 8)
    high_x = [odd_x == 0, odd_x == 1]
    high_y = [odd_y == 0, odd_y == 1]
    x_at = [jnp.where(h, HALO + block_x, 0) for h in high_x]
    y_at = [
        pl.multiple_of(jnp.where(h, own + block_y, own - HALO), 8) for h in high_y
    ]
    near_x = [jnp.where(h, 0, HALO // 2) for h in high_x]
    near_y = [
        pl.multiple_of(jnp.where(h, own + block_y, own - HALO // 2), 8) for h in high_y
    ]
    far_y = [
        pl.multiple_of(jnp.where(h, own + block_y + HALO // 2, own - HALO), 8)
        for h in high_y
    ]
    half = HALO // 2
    copies = []

    def fetch(src, dst):
        copy = pltpu.make_async_copy(src, dst, sems.at[len(copies)])
        copy.start()
        copies.append(copy)

    y_count = speed_y.shape[0]
    corners = (corners_now, corners_prev)
    own_rows = pl.ds(own, block_y)
    fetch(speed, near.at[pl.ds(HALO, block_x), own_rows])
    for e in range(2):
        fetch(speed_x[e], near.at[pl.ds(x_at[e], block_x), own_rows])
    for f in range(y_count):
        at = pl.ds(y_at[f], HALO)
        fetch(speed_y.at[f], near.at[pl.ds(HALO, block_x), at])
        for e in range(2):
            fetch(speed_xy.at[f, e], near.at[pl.ds(x_at[e], block_x), at])
    speed_copies = len(copies)
    fetch(now, now_ext.at[:, pl.ds(HALO, block_x), own_rows])
    fetch(prev, prev_ext.at[:, pl.ds(HALO, block_x), own_rows])
    for e in range(2):
        at = pl.ds(x_at[e], block_x)
        fetch(now_x[e], now_ext.at[:, at, own_rows])
        fetch(prev_x[e], prev_ext.at[:, at, own_rows])
    for f in range(y_count):
        at = pl.ds(y_at[f], HALO)
        fetch(sides.at[f, 0], now_ext.at[:, pl.ds(HALO, block_x), at])
        fetch(sides.at[f, 1], prev_ext.at[:, pl.ds(HALO, block_x), at])
        for e in range(2):
            at_near = pl.ds(x_at[e] + near_x[e], half)
            at_far = pl.ds(x_at[e] + half - near_x[e], half)
            for k, ext in enumerate((now_ext, prev_ext)):
                fetch(
                    corners[k].at[f, e, :, :, pl.ds(0, HALO)],
                    ext.at[:, at_near, at],
                )
                fetch(
                    corners[k].at[f, e, :, :, pl.ds(HALO, half)],
                    ext.at[:, at_far, pl.ds(near_y[f], half)],
                )

    blank = jnp.zeros((PAD, now_ext.shape[3]), jnp.float32)
    for ext in (now_ext, prev_ext):
        for s in range(shots):

            def clear(x, _):
                ext[s, x, pl.ds(0, PAD)] = blank
                ext[s, x, pl.ds(rows - PAD, PAD)] = blank
                return 0

            lax.fori_loop(0, planes, clear, 0)
            for f in range(y_count):
                for e in range(2):

                    def clear_far(x, _):
                        ext[s, x_at[e] + half - near_x[e] + x, pl.ds(far_y[f], half)] = blank
                        return 0

                    lax.fori_loop(0, half, clear_far, 0)

    def depth_in(cell, total):
        inside = (cell >= 0) & (cell < total)
        depth = jnp.maximum(
            block_x - jnp.minimum(cell + 1, total - cell), 0
        ).astype(jnp.float32) / block_x
        return inside, depth

    x_first = column * block_x - HALO
    y_first = row * block_y - own
    shape = (rows, now_ext.shape[3])
    y_in, y_depth = depth_in(lax.broadcasted_iota(jnp.int32, shape, 0) + y_first, total_y)
    y_part = y_depth * y_depth

    for k in range(shots * STEPS):
        samples[k] = jnp.zeros(samples.shape[1:], jnp.float32)
    for copy in copies[:speed_copies]:
        copy.wait()

    def prepare(x, _):
        x_in, x_depth = depth_in(jnp.full(shape, x + x_first, jnp.int32), total_x)
        inverse = 1.0 / (1.0 + damp_peak * (x_depth * x_depth + y_part))
        inverse = jnp.where(x_in & y_in, inverse, 0.0)
        v = near[x]
        near[x] = jnp.where(x_in & y_in, inverse * (v * v) * near_weight, 0.0)
        twice[x] = 2.0 * inverse
        return 0

    lax.fori_loop(2, planes - 2, prepare, 0, unroll=2)
    for copy in copies[speed_copies:]:
        copy.wait()

    depth = now_ext.shape[3]
    gap = lax.broadcasted_iota(jnp.int32, (depth, depth), 0) - lax.broadcasted_iota(jnp.int32, (depth, depth), 1)
    gap = jnp.abs(gap)
    band = jnp.where(gap == 0, centre_part, jnp.where(gap == 1, 1.0, jnp.where(gap == 2, far_part, 0.0)))
    band = band.astype(jnp.bfloat16)
    band = jnp.concatenate([band, band], axis=0)
    lane_row = lax.broadcasted_iota(jnp.int32, (1, depth), 1)

    cur, old = now_ext, prev_ext
    for step in range(1, STEPS + 1):
        reach = 2 * (STEPS - step)
        side = -(-reach // 8)
        if ny == 2:
            first = pl.multiple_of(own - 8 * side * odd_y, 8)
            tiles = block_y // 8 + side
        else:
            first = pl.multiple_of(own - 8 * side, 8)
            tiles = block_y // 8 + 2 * side

        size = 8 * tiles

        def plane(g, _, cur=cur, old=old, first=first, tiles=tiles, size=size, step=step):
            x = 2 * step + GROUP * g
            along = []
            for s in range(shots):
                c = cur[s, pl.ds(x, GROUP), pl.ds(first, size)].reshape(GROUP * size, depth)
                head = c.astype(jnp.bfloat16)
                rest = (c - head.astype(jnp.float32)).astype(jnp.bfloat16)
                parts = jnp.concatenate([head, rest], axis=1)
                out = jnp.dot(parts, band, preferred_element_type=jnp.float32)
                along.append(out.reshape(GROUP, size, depth))
            for s in range(shots):
                for j in range(tiles):
                    base = first + 8 * j
                    at = pl.ds(pl.multiple_of(base, 8), 8)
                    n = [near[x + i, at] for i in range(GROUP)]
                    a = [twice[x + i, at] for i in range(GROUP)]
                    c = [cur[s, x + i - 2, at] for i in range(GROUP + 4)]
                    out = []
                    for i in range(GROUP):
                        m = c[i + 2]
                        close = (c[i + 1] + c[i + 3]) + (cur[s, x + i, pl.ds(base - 1, 8)] + cur[s, x + i, pl.ds(base + 1, 8)])
                        wide = (c[i] + c[i + 4]) + (cur[s, x + i, pl.ds(base - 2, 8)] + cur[s, x + i, pl.ds(base + 2, 8)])
                        p = old[s, x + i, at]
                        lap = along[s][i, 8 * j : 8 * j + 8] + close + far_part * wide
                        out.append(p + a[i] * (m - p) + n[i] * lap)
                    for i in range(GROUP):
                        old[s, x + i, at] = out[i]
            return 0

        lax.fori_loop(0, (planes - 4 * step) // GROUP, plane, 0)

        for s in range(shots):
            sx = sources[s, 0] - x_first
            sy = sources[s, 1] - y_first
            sz = sources[s, 2]
            amplitude = amplitudes[s, step - 1]
            inside = (
                (sx >= 2 * step)
                & (sx < planes - 2 * step)
                & (sy >= first)
                & (sy < first + 8 * tiles)
            )

            @pl.when(inside)
            def _(old=old, s=s, sx=sx, sy=sy, sz=sz, amplitude=amplitude):
                at = pl.ds(sy, 1)
                old[s, sx, at] += jnp.where(lane_row == sz, (0.5 * amplitude) * twice[sx, at], 0.0)

        cur, old = old, cur

        def take(g, _, cur=cur, step=step):
            found = []
            for i in range(BATCH):
                at = 1 + 3 * (BATCH * g + i)
                cell, z = local_list[at + 1], local_list[at + 2]
                x = HALO + cell // block_y
                y = own + cell % block_y
                for s in range(shots):
                    found.append(jnp.where(lane_row == z, cur[s, x, pl.ds(y, 1)], 0.0))
            for i in range(BATCH):
                r = local_list[1 + 3 * (BATCH * g + i)]
                for s in range(shots):
                    samples[s * STEPS + step - 1, pl.ds(r, 1)] = found[i * shots + s]
            return 0

        lax.fori_loop(0, (local_list[0] + BATCH - 1) // BATCH, take, 0)
        if step >= STEPS - 1:
            out = out_prev if step == STEPS - 1 else out_now
            copy = pltpu.make_async_copy(
                cur.at[:, pl.ds(HALO, block_x), own_rows],
                out,
                out_sems.at[step - STEPS + 1],
            )
            copy.start()
            if step == STEPS - 1:
                first_out = copy
            else:
                last_out = copy

    total = partial.shape[2]
    for k in range(shots * STEPS):
        values = jnp.sum(samples[k, pl.ds(0, total)], axis=1)
        for copy_to in range(partial.shape[0]):
            partial[copy_to, k] = values
    first_out.wait()
    last_out.wait()


def window(sizes, starts, sources, amplitudes, local_list, recs, now, prev, now_x, prev_x, sides, corners, speed, speed_x, speed_y, speed_xy, copies):
    block_x, block_y, total_x, total_y, ny = sizes
    shots, _, _, depth = now.shape
    planes = block_x + 2 * HALO
    rows = block_y + (HALO if ny == 2 else 2 * HALO) + 2 * PAD

    def kernel(starts, sources, amplitudes, local_list, now, prev, n0, n1, p0, p1, sides, corners_now, corners_prev, speed, v0, v1, *rest):
        window_kernel(
            sizes, starts, sources, amplitudes, local_list, now, prev,
            (n0, n1), (p0, p1), sides, corners_now, corners_prev, speed, (v0, v1), *rest,
        )

    return pl.pallas_call(
        kernel,
        out_shape=(
            jax.ShapeDtypeStruct(now.shape, now.dtype),
            jax.ShapeDtypeStruct(now.shape, now.dtype),
            jax.ShapeDtypeStruct((copies, shots * STEPS, recs), now.dtype),
        ),
        in_specs=[SMEM] * 4 + [ANY] * 14,
        out_specs=(ANY, ANY, VMEM),
        scratch_shapes=[
            pltpu.VMEM((2 * shots + 2, planes, rows, depth), jnp.float32),
            pltpu.VMEM((shots * STEPS, recs + 8, depth), jnp.float32),
            pltpu.SemaphoreType.DMA((48,)),
            pltpu.SemaphoreType.DMA((2,)),
        ],
        compiler_params=pltpu.CompilerParams(vmem_limit_bytes=40 * 2**20),
        name="wave_window",
    )(
        starts, sources, amplitudes, local_list, now, prev, *now_x, *prev_x,
        sides, *corners, speed, *speed_x, speed_y, speed_xy,
    )


def local(model_tiles, owner_map, offsets, field_now, field_prev, sources, wavelet, receivers):
    block_x, block_y, depth = model_tiles.shape
    nx, ny, groups = lax.axis_size("gx"), lax.axis_size("gy"), lax.axis_size("sy")
    column, row, core = lax.axis_index("gx"), lax.axis_index("gy"), lax.axis_index("core")
    shot_row = lax.axis_index("sy")
    total_x, total_y = block_x * nx, block_y * ny
    now, prev = field_now[0], field_prev[0]
    x_perms = [pairs(nx, 0), pairs(nx, 1)]
    y_perms = [pairs(ny, f) for f in range(2 if ny > 2 else 1)]
    places = jnp.stack([column, row, jnp.int32(nx), core]).astype(jnp.int32)

    now_x = [lax.ppermute(now, "gx", perm) for perm in x_perms]
    spread = lax.all_to_all(model_tiles, ("sy", "gx"), 0, 0, tiled=True)
    other = lax.ppermute(spread, "core", [(0, 1), (1, 0)])
    prev_x = [lax.ppermute(prev, "gx", perm) for perm in x_perms]
    sides = jnp.stack(
        [lax.ppermute(pack_sides(f, places, now, prev), "gy", perm) for f, perm in enumerate(y_perms)]
    )
    corners = [
        jnp.stack(
            [lax.ppermute(pack_corners(f, places, blocks), "gy", perm) for f, perm in enumerate(y_perms)]
        )
        for blocks in (now_x, prev_x)
    ]

    shifts = jnp.zeros((groups,), jnp.int32)
    for turn in range(groups):
        came = offsets if turn == 0 else lax.ppermute(
            offsets, "sy", [(i, (i + turn) % groups) for i in range(groups)]
        )
        at = (shot_row - turn) % groups
        shifts = jnp.where(jnp.arange(groups) == at, came, shifts)
    columns = (shifts[:, None] + jnp.arange(nx, dtype=jnp.int32)[None, :]).reshape(-1)
    stored_in, local_list = prepare(block_x, block_y, places, owner_map, columns, receivers[0].T)
    targets = groups * nx
    slice_shape = (targets, block_x // targets, block_y, depth)
    picked = pick(stored_in, places, spread.reshape(slice_shape), other.reshape(slice_shape))
    speed = lax.all_to_all(picked.reshape(model_tiles.shape), ("sy", "gx"), 0, 0, tiled=True)
    speed_x = [lax.ppermute(speed, "gx", perm) for perm in x_perms]
    speed_y, speed_xy = [], []
    for f, perm in enumerate(y_perms):
        start = jnp.where(row % 2 == f, block_y - HALO, 0)
        part = lax.dynamic_slice_in_dim(speed, start, HALO, axis=1)
        speed_y.append(lax.ppermute(part, "gy", perm))
        speed_xy.append(
            jnp.stack([lax.ppermute(part, ("gx", "gy"), joint(x_perm, perm, ny)) for x_perm in x_perms])
        )

    out_now, out_prev, partial = window(
        (block_x, block_y, total_x, total_y, ny),
        places, sources[0], wavelet[0], local_list, receivers.shape[1],
        now, prev, now_x, prev_x, sides, corners,
        speed, speed_x, jnp.stack(speed_y), jnp.stack(speed_xy), nx * ny,
    )
    gathered = lax.all_to_all(partial, ("gx", "gy"), 0, 0, tiled=True)
    shots = now.shape[0]
    traces = jnp.sum(gathered, axis=0).reshape(shots, STEPS, -1).transpose(0, 2, 1)
    return (out_now[None], out_prev[None], traces[None])


def solution(mesh):
    shape = dict(zip(mesh.axis_names, mesh.devices.shape))
    cores = 2 if shape["shot"] % 2 == 0 else 1
    fine = Mesh(
        mesh.devices.reshape(shape["shot"] // cores, cores, shape["gx"], shape["gy"]),
        ("sy", "core", "gx", "gy"),
    )
    shot = ("sy", "core")
    field = P(shot, None, "gx", "gy", None)
    return jax.shard_map(
        local,
        mesh=fine,
        in_specs=(
            P(("sy", "core", "gx"), "gy", None),
            P(),
            P(shot),
            field,
            field,
            P(shot, None, None),
            P(shot, None, None),
            P(shot, None, None),
        ),
        out_specs=(field, field, P(shot, None, None, None)),
        check_vma=False,
    )
```

```python
import functools

import jax
import jax.numpy as jnp
from jax import lax
from jax.experimental import pallas as pl
from jax.experimental.pallas import tpu as pltpu
from jax.sharding import Mesh
from jax.sharding import PartitionSpec as P

STEPS = 8
HALO = 2 * STEPS
PAD = 8
HALF = HALO // 2
REACH_NOW = (HALF - 1, HALF)
REACH_PREV = (HALF - 3, HALF)
GROUP = 4
BATCH = 4

near_weight = 4.0 / 3.0
centre_part = -7.5 * 0.75
far_part = -1.0 / 16.0
damp_peak = 0.3

SMEM = pl.BlockSpec(memory_space=pltpu.SMEM)
ANY = pl.BlockSpec(memory_space=pl.ANY)
VMEM = pl.BlockSpec(memory_space=pltpu.VMEM)


def pairs(count, parity):
    return [
        pair
        for i in range(parity, count - 1, 2)
        for pair in ((i, i + 1), (i + 1, i))
    ]


def joint(first, second, count):
    return [(a * count + b, c * count + d) for a, c in first for b, d in second]


def list_kernel(block_x, block_y, receivers, local_list):
    x_first, y_first = lax.axis_index("gx") * block_x, lax.axis_index("gy") * block_y
    total = receivers.shape[1]
    batch = 8

    def body(g, count):
        for i in range(batch):
            r = g * batch + i
            x = receivers[0, r] - x_first
            y = receivers[1, r] - y_first
            inside = (x >= 0) & (x < block_x) & (y >= 0) & (y < block_y)
            local_list[1 + 3 * count] = r
            local_list[2 + 3 * count] = x * block_y + y
            local_list[3 + 3 * count] = receivers[2, r]
            count = count + inside.astype(jnp.int32)
        return count

    count = lax.fori_loop(0, total // batch, body, jnp.int32(0))
    local_list[0] = count
    for i in range(BATCH):
        local_list[1 + 3 * (count + i)] = total
        local_list[2 + 3 * (count + i)] = 0
        local_list[3 + 3 * (count + i)] = 0


def list_receivers(block_x, block_y, receivers):
    total = receivers.shape[1]
    return pl.pallas_call(
        functools.partial(list_kernel, block_x, block_y),
        out_shape=jax.ShapeDtypeStruct((3 * (total + BATCH) + 8,), jnp.int32),
        in_specs=[SMEM],
        out_specs=SMEM,
        name="list_receivers",
    )(receivers)


def pick_kernel(across, groups, owner_map, *refs):
    shifts, (stored, other, out, sems) = refs[:groups], refs[groups:]
    core, mine = lax.axis_index("core"), lax.axis_index("sy")
    copies = []
    for turn in range(groups):
        group = lax.rem(mine + groups - turn, groups)
        for z in range(across):
            block = owner_map[shifts[turn][0] + z]
            owner_core = lax.rem(block // across, 2)
            row = (block // (2 * across)) * across + lax.rem(block, across)
            t = group * across + z
            here = pltpu.make_async_copy(stored.at[row], out.at[t], sems.at[len(copies)])
            there = pltpu.make_async_copy(other.at[row], out.at[t], sems.at[len(copies)])
            pl.when(owner_core == core)(here.start)
            pl.when(owner_core != core)(there.start)
            copies.append(here)
    for copy in copies:
        copy.wait()


def pick(across, shifts, owner_map, stored, other):
    targets = stored.shape[0]
    return pl.pallas_call(
        functools.partial(pick_kernel, across, len(shifts)),
        out_shape=jax.ShapeDtypeStruct(stored.shape, stored.dtype),
        in_specs=[SMEM] * (1 + len(shifts)) + [ANY, ANY],
        out_specs=VMEM,
        scratch_shapes=[pltpu.SemaphoreType.DMA((targets,))],
        name="pick_slices",
    )(owner_map, *shifts, stored, other)


def corner_kernel(block_y, parity_y, reach, first, second, out, sems):
    near, far = reach
    block_x = first.shape[1]
    odd_x, odd_y = lax.rem(lax.axis_index("gx"), 2), lax.rem(lax.axis_index("gy"), 2)
    above = odd_y == parity_y
    start = pl.multiple_of(jnp.where(above, block_y - HALO, 0), 8)
    near_start = pl.multiple_of(jnp.where(above, block_y - HALF, 0), 8)
    copies = []
    for e, block in enumerate((first, second)):
        high = odd_x == e
        copies.append(
            pltpu.make_async_copy(
                block.at[:, pl.ds(jnp.where(high, 0, block_x - near), near), pl.ds(start, HALO)],
                out.at[e, :, pl.ds(0, near)],
                sems.at[2 * e],
            )
        )
        for k in range(2):
            first_plane = jnp.where(high, near, block_x - near - far) + k * (far // 2)
            copies.append(
                pltpu.make_async_copy(
                    block.at[:, pl.ds(first_plane, far // 2), pl.ds(near_start, HALF)],
                    out.at[e, :, pl.ds(near, far // 2), pl.ds(k * HALF, HALF)],
                    sems.at[4 + 2 * e + k],
                )
            )
    for copy in copies:
        copy.start()
    for copy in copies:
        copy.wait()


def pack_corners(parity_y, reach, blocks):
    shots, _, block_y, depth = blocks[0].shape
    near, far = reach
    return pl.pallas_call(
        functools.partial(corner_kernel, block_y, parity_y, reach),
        out_shape=jax.ShapeDtypeStruct((2, shots, near + far // 2, HALO, depth), jnp.float32),
        in_specs=[ANY, ANY],
        out_specs=VMEM,
        scratch_shapes=[pltpu.SemaphoreType.DMA((8,))],
        name="pack_corners",
    )(*blocks)


def side_kernel(block_y, parity_y, now, prev, out, sems):
    above = lax.rem(lax.axis_index("gy"), 2) == parity_y
    start = pl.multiple_of(jnp.where(above, block_y - HALO, 0), 8)
    copies = [
        pltpu.make_async_copy(block.at[:, :, pl.ds(start, HALO)], out.at[k], sems.at[k])
        for k, block in enumerate((now, prev))
    ]
    for copy in copies:
        copy.start()
    for copy in copies:
        copy.wait()


def pack_sides(parity_y, now, prev):
    shots, block_x, block_y, depth = now.shape
    return pl.pallas_call(
        functools.partial(side_kernel, block_y, parity_y),
        out_shape=jax.ShapeDtypeStruct((2, shots, block_x, HALO, depth), jnp.float32),
        in_specs=[ANY, ANY],
        out_specs=VMEM,
        scratch_shapes=[pltpu.SemaphoreType.DMA((2,))],
        name="pack_sides",
    )(now, prev)


def window_kernel(
    sizes,
    sources,
    amplitudes,
    local_list,
    now,
    prev,
    now_x,
    prev_x,
    sides,
    corners_now,
    corners_prev,
    speed,
    speed_x,
    speed_y,
    speed_xy,
    out_now,
    out_prev,
    partial,
    ext_all,
    samples,
    sems,
    out_sems,
):
    block_x, block_y, total_x, total_y, ny = sizes
    half_way = (ext_all.shape[0] - 2) // 2
    now_ext, prev_ext = ext_all.at[pl.ds(0, half_way)], ext_all.at[pl.ds(half_way, half_way)]
    near, twice = ext_all.at[2 * half_way], ext_all.at[2 * half_way + 1]
    rows = now_ext.shape[2]
    planes = now_ext.shape[1]
    shots = now_ext.shape[0]
    column, row = lax.axis_index("gx"), lax.axis_index("gy")
    odd_x, odd_y = lax.rem(column, 2), lax.rem(row, 2)
    own = pl.multiple_of(PAD + (HALO * odd_y if ny == 2 else HALO), 8)
    high_x = [odd_x == 0, odd_x == 1]
    high_y = [odd_y == 0, odd_y == 1]
    x_at = [jnp.where(h, HALO + block_x, 0) for h in high_x]
    y_at = [
        pl.multiple_of(jnp.where(h, own + block_y, own - HALO), 8) for h in high_y
    ]
    near_y = [
        pl.multiple_of(jnp.where(h, own + block_y, own - HALF), 8) for h in high_y
    ]
    y_count = len(speed_y)
    blank = jnp.zeros((PAD, now_ext.shape[3]), jnp.float32)

    def clear(x, _):
        for s in range(2 * shots):
            ext_all[s, x, pl.ds(0, PAD)] = blank
            ext_all[s, x, pl.ds(rows - PAD, PAD)] = blank
        return 0

    lax.fori_loop(0, planes, clear, 0)
    for f in range(y_count):
        for e in range(2):

            def clear_corner(x, _):
                for s in range(2 * shots + 1):
                    for k in range(HALO // PAD):
                        ext_all[s, x_at[e] + x, pl.ds(y_at[f] + PAD * k, PAD)] = blank
                return 0

            lax.fori_loop(0, HALO, clear_corner, 0)

    copies = []

    def fetch(src, dst):
        copy = pltpu.make_async_copy(src, dst, sems.at[len(copies)])
        copy.start()
        copies.append(copy)


    def place_corner(ext, packed, reach, e, f):
        near, far = reach
        lead = pl.ds(jnp.where(high_x[e], HALO + block_x, HALO - near), near)
        fetch(packed.at[:, pl.ds(0, near)], ext.at[:, lead, pl.ds(y_at[f], HALO)])
        for k in range(2):
            first_plane = jnp.where(high_x[e], HALO + block_x + near, HALO - near - far)
            fetch(
                packed.at[:, pl.ds(near, far // 2), pl.ds(k * HALF, HALF)],
                ext.at[:, pl.ds(first_plane + k * (far // 2), far // 2), pl.ds(near_y[f], HALF)],
            )

    own_rows = pl.ds(own, block_y)
    fetch(speed, near.at[pl.ds(HALO, block_x), own_rows])
    for e in range(2):
        fetch(speed_x[e], near.at[pl.ds(x_at[e], block_x), own_rows])
    for f in range(y_count):
        at = pl.ds(y_at[f], HALO)
        fetch(speed_y[f], near.at[pl.ds(HALO, block_x), at])
        for e in range(2):
            fetch(speed_xy[2 * f + e], near.at[pl.ds(x_at[e], block_x), at])
    speed_copies = len(copies)
    fetch(now, now_ext.at[:, pl.ds(HALO, block_x), own_rows])
    fetch(prev, prev_ext.at[:, pl.ds(HALO, block_x), own_rows])
    for e in range(2):
        at = pl.ds(x_at[e], block_x)
        fetch(now_x[e], now_ext.at[:, at, own_rows])
        fetch(prev_x[e], prev_ext.at[:, at, own_rows])
    for f in range(y_count):
        at = pl.ds(y_at[f], HALO)
        fetch(sides[f].at[0], now_ext.at[:, pl.ds(HALO, block_x), at])
        fetch(sides[f].at[1], prev_ext.at[:, pl.ds(HALO, block_x), at])
        for e in range(2):
            for ext, packed, reach in (
                (now_ext, corners_now, REACH_NOW),
                (prev_ext, corners_prev, REACH_PREV),
            ):
                place_corner(ext, packed[f].at[e], reach, e, f)

    def depth_in(cell, total):
        inside = (cell >= 0) & (cell < total)
        depth = jnp.maximum(
            block_x - jnp.minimum(cell + 1, total - cell), 0
        ).astype(jnp.float32) / block_x
        return inside, depth

    x_first = column * block_x - HALO
    y_first = row * block_y - own
    shape = (rows, now_ext.shape[3])
    y_in, y_depth = depth_in(lax.broadcasted_iota(jnp.int32, shape, 0) + y_first, total_y)
    y_part = y_depth * y_depth

    for k in range(shots * STEPS):
        samples[k] = jnp.zeros(samples.shape[1:], jnp.float32)
    for copy in copies[:speed_copies]:
        copy.wait()

    def prepare(x, _):
        x_in, x_depth = depth_in(jnp.full(shape, x + x_first, jnp.int32), total_x)
        inverse = 1.0 / (1.0 + damp_peak * (x_depth * x_depth + y_part))
        inverse = jnp.where(x_in & y_in, inverse, 0.0)
        v = near[x]
        near[x] = jnp.where(x_in & y_in, inverse * (v * v) * near_weight, 0.0)
        twice[x] = 2.0 * inverse
        return 0

    lax.fori_loop(2, planes - 2, prepare, 0, unroll=2)
    for copy in copies[speed_copies:]:
        copy.wait()

    depth = now_ext.shape[3]
    gap = lax.broadcasted_iota(jnp.int32, (depth, depth), 0) - lax.broadcasted_iota(jnp.int32, (depth, depth), 1)
    gap = jnp.abs(gap)
    band = jnp.where(gap == 0, centre_part, jnp.where(gap == 1, 1.0, jnp.where(gap == 2, far_part, 0.0)))
    band = band.astype(jnp.bfloat16)
    band = jnp.concatenate([band, band], axis=0)
    lane_row = lax.broadcasted_iota(jnp.int32, (1, depth), 1)

    cur, old = now_ext, prev_ext
    for step in range(1, STEPS + 1):
        reach = 2 * (STEPS - step)
        side = -(-reach // 8)
        if ny == 2:
            first = pl.multiple_of(own - 8 * side * odd_y, 8)
            tiles = block_y // 8 + side
        else:
            first = pl.multiple_of(own - 8 * side, 8)
            tiles = block_y // 8 + 2 * side

        size = 8 * tiles

        def plane(g, _, cur=cur, old=old, first=first, tiles=tiles, size=size, step=step):
            x = 2 * step + GROUP * g
            along = []
            for s in range(shots):
                c = cur[s, pl.ds(x, GROUP), pl.ds(first, size)].reshape(GROUP * size, depth)
                head = c.astype(jnp.bfloat16)
                rest = (c - head.astype(jnp.float32)).astype(jnp.bfloat16)
                parts = jnp.concatenate([head, rest], axis=1)
                out = jnp.dot(parts, band, preferred_element_type=jnp.float32)
                along.append(out.reshape(GROUP, size, depth))
            for s in range(shots):
                for j in range(tiles):
                    base = first + 8 * j
                    at = pl.ds(pl.multiple_of(base, 8), 8)
                    n = [near[x + i, at] for i in range(GROUP)]
                    a = [twice[x + i, at] for i in range(GROUP)]
                    c = [cur[s, x + i - 2, at] for i in range(GROUP + 4)]
                    out = []
                    for i in range(GROUP):
                        m = c[i + 2]
                        close = (c[i + 1] + c[i + 3]) + (cur[s, x + i, pl.ds(base - 1, 8)] + cur[s, x + i, pl.ds(base + 1, 8)])
                        wide = (c[i] + c[i + 4]) + (cur[s, x + i, pl.ds(base - 2, 8)] + cur[s, x + i, pl.ds(base + 2, 8)])
                        p = old[s, x + i, at]
                        lap = along[s][i, 8 * j : 8 * j + 8] + close + far_part * wide
                        out.append(p + a[i] * (m - p) + n[i] * lap)
                    for i in range(GROUP):
                        old[s, x + i, at] = out[i]
            return 0

        lax.fori_loop(0, (planes - 4 * step) // GROUP, plane, 0)

        for s in range(shots):
            sx = sources[s, 0] - x_first
            sy = sources[s, 1] - y_first
            sz = sources[s, 2]
            amplitude = amplitudes[s, step - 1]
            inside = (
                (sx >= 2 * step)
                & (sx < planes - 2 * step)
                & (sy >= first)
                & (sy < first + 8 * tiles)
            )

            @pl.when(inside)
            def _(old=old, s=s, sx=sx, sy=sy, sz=sz, amplitude=amplitude):
                at = pl.ds(sy, 1)
                old[s, sx, at] += jnp.where(lane_row == sz, (0.5 * amplitude) * twice[sx, at], 0.0)

        cur, old = old, cur

        def take(g, _, cur=cur, step=step):
            found = []
            for i in range(BATCH):
                at = 1 + 3 * (BATCH * g + i)
                cell, z = local_list[at + 1], local_list[at + 2]
                x = HALO + cell // block_y
                y = own + cell % block_y
                for s in range(shots):
                    found.append(jnp.where(lane_row == z, cur[s, x, pl.ds(y, 1)], 0.0))
            for i in range(BATCH):
                r = local_list[1 + 3 * (BATCH * g + i)]
                for s in range(shots):
                    samples[s * STEPS + step - 1, pl.ds(r, 1)] = found[i * shots + s]
            return 0

        lax.fori_loop(0, (local_list[0] + BATCH - 1) // BATCH, take, 0)
        if step >= STEPS - 1:
            out = out_prev if step == STEPS - 1 else out_now
            copy = pltpu.make_async_copy(
                cur.at[:, pl.ds(HALO, block_x), own_rows],
                out,
                out_sems.at[step - STEPS + 1],
            )
            copy.start()
            if step == STEPS - 1:
                first_out = copy
            else:
                last_out = copy

    total = partial.shape[2]
    for k in range(shots * STEPS):
        values = jnp.sum(samples[k, pl.ds(0, total)], axis=1)
        for copy_to in range(partial.shape[0]):
            partial[copy_to, k] = values
    first_out.wait()
    last_out.wait()


def window(sizes, sources, amplitudes, local_list, recs, now, prev, now_x, prev_x, sides, corners, speed, speed_x, speed_y, speed_xy, copies):
    block_x, block_y, total_x, total_y, ny = sizes
    shots, _, _, depth = now.shape
    planes = block_x + 2 * HALO
    rows = block_y + (HALO if ny == 2 else 2 * HALO) + 2 * PAD

    count = len(speed_y)
    parts = [now, prev, *now_x, *prev_x, *sides, *corners[0], *corners[1], speed, *speed_x, *speed_y, *speed_xy]

    def kernel(sources, amplitudes, local_list, *refs):
        groups = []
        for size in (1, 1, 2, 2, count, count, count, 1, 2, count, 2 * count):
            groups.append(refs[0] if size == 1 and len(groups) in (0, 1, 7) else refs[:size])
            refs = refs[size:]
        window_kernel(sizes, sources, amplitudes, local_list, *groups, *refs)

    return pl.pallas_call(
        kernel,
        out_shape=(
            jax.ShapeDtypeStruct(now.shape, now.dtype),
            jax.ShapeDtypeStruct(now.shape, now.dtype),
            jax.ShapeDtypeStruct((copies, shots * STEPS, recs), now.dtype),
        ),
        in_specs=[SMEM] * 3 + [ANY] * len(parts),
        out_specs=(ANY, ANY, VMEM),
        scratch_shapes=[
            pltpu.VMEM((2 * shots + 2, planes, rows, depth), jnp.float32),
            pltpu.VMEM((shots * STEPS, recs + 8, depth), jnp.float32),
            pltpu.SemaphoreType.DMA((64,)),
            pltpu.SemaphoreType.DMA((2,)),
        ],
        compiler_params=pltpu.CompilerParams(vmem_limit_bytes=40 * 2**20),
        name="wave_window",
    )(
        sources, amplitudes, local_list, *parts
    )


def local(model_tiles, owner_map, offsets, field_now, field_prev, sources, wavelet, receivers):
    block_x, block_y, depth = model_tiles.shape
    nx, ny, groups = lax.axis_size("gx"), lax.axis_size("gy"), lax.axis_size("sy")
    row = lax.axis_index("gy")
    total_x, total_y = block_x * nx, block_y * ny
    now, prev = field_now[0], field_prev[0]
    x_perms = [pairs(nx, 0), pairs(nx, 1)]
    y_perms = [pairs(ny, f) for f in range(2 if ny > 2 else 1)]
    spread = lax.all_to_all(model_tiles, ("sy", "gx"), 0, 0, tiled=True)
    now_x = [lax.ppermute(now, "gx", perm) for perm in x_perms]
    packed = [pack_sides(f, now, prev) for f in range(len(y_perms))]
    shifts = [offsets] + [
        lax.ppermute(offsets, "sy", [(i, (i + turn) % groups) for i in range(groups)])
        for turn in range(1, groups)
    ]
    sides = [lax.ppermute(part, "gy", perm) for part, perm in zip(packed, y_perms)]
    spread, packed, shifts, later = lax.optimization_barrier((spread, packed, shifts, prev))
    other = lax.ppermute(spread, "core", [(0, 1), (1, 0)])
    prev_x = [lax.ppermute(later, "gx", perm) for perm in x_perms]
    local_list = list_receivers(block_x, block_y, receivers[0].T)

    def cut_corners(blocks, reach):
        return [pack_corners(f, reach, blocks) for f in range(len(y_perms))]

    def swap_corners(packed):
        return [lax.ppermute(part, "gy", perm) for part, perm in zip(packed, y_perms)]


    targets = groups * nx
    slice_shape = (targets, block_x // targets, block_y, depth)
    picked = pick(nx, shifts, owner_map, spread.reshape(slice_shape), other.reshape(slice_shape))
    picked, now_x, sides = lax.optimization_barrier((picked, now_x, sides))
    cut_now = cut_corners(now_x, REACH_NOW)
    corners_now = swap_corners(cut_now)
    speed = lax.all_to_all(picked.reshape(model_tiles.shape), ("sy", "gx"), 0, 0, tiled=True)
    speed, prev_x, corners_now, local_list = lax.optimization_barrier((speed, prev_x, corners_now, local_list))
    corners = (corners_now, swap_corners(cut_corners(prev_x, REACH_PREV)))
    speed_x = [lax.ppermute(speed, "gx", perm) for perm in x_perms]
    speed_y, speed_xy = [], []
    for f, perm in enumerate(y_perms):
        start = jnp.where(row % 2 == f, block_y - HALO, 0)
        part = lax.dynamic_slice_in_dim(speed, start, HALO, axis=1)
        speed_y.append(lax.ppermute(part, "gy", perm))
        speed_xy += [lax.ppermute(part, ("gx", "gy"), joint(x_perm, perm, ny)) for x_perm in x_perms]

    out_now, out_prev, partial = window(
        (block_x, block_y, total_x, total_y, ny),
        sources[0], wavelet[0], local_list, receivers.shape[1],
        now, prev, now_x, prev_x, sides, corners,
        speed, speed_x, speed_y, speed_xy, nx * ny,
    )
    gathered = lax.all_to_all(partial, ("gx", "gy"), 0, 0, tiled=True)
    shots = now.shape[0]
    traces = jnp.sum(gathered, axis=0).reshape(shots, STEPS, -1).transpose(0, 2, 1)
    return (out_now[None], out_prev[None], traces[None])


def solution(mesh):
    shape = dict(zip(mesh.axis_names, mesh.devices.shape))
    cores = 2 if shape["shot"] % 2 == 0 else 1
    fine = Mesh(
        mesh.devices.reshape(shape["shot"] // cores, cores, shape["gx"], shape["gy"]),
        ("sy", "core", "gx", "gy"),
    )
    shot = ("sy", "core")
    field = P(shot, None, "gx", "gy", None)
    return jax.shard_map(
        local,
        mesh=fine,
        in_specs=(
            P(("sy", "core", "gx"), "gy", None),
            P(),
            P(shot),
            field,
            field,
            P(shot, None, None),
            P(shot, None, None),
            P(shot, None, None),
        ),
        out_specs=(field, field, P(shot, None, None, None)),
        check_vma=False,
    )
```

```python
import functools

import jax
import jax.numpy as jnp
from jax import lax
from jax.experimental import pallas as pl
from jax.experimental.pallas import tpu as pltpu
from jax.sharding import Mesh
from jax.sharding import PartitionSpec as P

STEPS = 8
HALO = 2 * STEPS
PAD = 8
HALF = HALO // 2
REACH_NOW = (HALF - 1, HALF)
REACH_PREV = (HALF - 3, HALF)
GROUP = 4
BATCH = 4

near_weight = 4.0 / 3.0
centre_part = -7.5 * 0.75
far_part = -1.0 / 16.0
damp_peak = 0.3

SMEM = pl.BlockSpec(memory_space=pltpu.SMEM)
ANY = pl.BlockSpec(memory_space=pl.ANY)
SMALL = 4 * 2**20
VMEM = pl.BlockSpec(memory_space=pltpu.VMEM)


def pairs(count, parity):
    return [
        pair
        for i in range(parity, count - 1, 2)
        for pair in ((i, i + 1), (i + 1, i))
    ]


def joint(first, second, count):
    return [(a * count + b, c * count + d) for a, c in first for b, d in second]


def list_kernel(block_x, block_y, receivers, local_list):
    x_first, y_first = lax.axis_index("gx") * block_x, lax.axis_index("gy") * block_y
    total = receivers.shape[1]
    batch = 8

    def body(g, count):
        for i in range(batch):
            r = g * batch + i
            x = receivers[0, r] - x_first
            y = receivers[1, r] - y_first
            inside = (x >= 0) & (x < block_x) & (y >= 0) & (y < block_y)
            local_list[1 + 3 * count] = r
            local_list[2 + 3 * count] = x * block_y + y
            local_list[3 + 3 * count] = receivers[2, r]
            count = count + inside.astype(jnp.int32)
        return count

    count = lax.fori_loop(0, total // batch, body, jnp.int32(0))
    local_list[0] = count
    for i in range(BATCH):
        local_list[1 + 3 * (count + i)] = total
        local_list[2 + 3 * (count + i)] = 0
        local_list[3 + 3 * (count + i)] = 0


def list_receivers(block_x, block_y, receivers):
    total = receivers.shape[1]
    return pl.pallas_call(
        functools.partial(list_kernel, block_x, block_y),
        out_shape=jax.ShapeDtypeStruct((3 * (total + BATCH) + 8,), jnp.int32),
        in_specs=[SMEM],
        out_specs=SMEM,
        compiler_params=pltpu.CompilerParams(vmem_limit_bytes=SMALL),
        name="list_receivers",
    )(receivers)


def pick_kernel(across, groups, owner_map, *refs):
    shifts, (stored, other, out, sems) = refs[:groups], refs[groups:]
    core, mine = lax.axis_index("core"), lax.axis_index("sy")
    copies = []
    for turn in range(groups):
        group = lax.rem(mine + groups - turn, groups)
        for z in range(across):
            block = owner_map[shifts[turn][0] + z]
            owner_core = lax.rem(block // across, 2)
            row = (block // (2 * across)) * across + lax.rem(block, across)
            t = group * across + z
            here = pltpu.make_async_copy(stored.at[row], out.at[t], sems.at[len(copies)])
            there = pltpu.make_async_copy(other.at[row], out.at[t], sems.at[len(copies)])
            pl.when(owner_core == core)(here.start)
            pl.when(owner_core != core)(there.start)
            copies.append(here)
    for copy in copies:
        copy.wait()


def pick(across, shifts, owner_map, stored, other):
    targets = stored.shape[0]
    return pl.pallas_call(
        functools.partial(pick_kernel, across, len(shifts)),
        out_shape=jax.ShapeDtypeStruct(stored.shape, stored.dtype),
        in_specs=[SMEM] * (1 + len(shifts)) + [ANY, ANY],
        out_specs=VMEM,
        scratch_shapes=[pltpu.SemaphoreType.DMA((targets,))],
        compiler_params=pltpu.CompilerParams(vmem_limit_bytes=SMALL),
        name="pick_slices",
    )(owner_map, *shifts, stored, other)


def corner_kernel(block_y, parity_y, reach, first, second, out, sems):
    near, far = reach
    block_x = first.shape[1]
    odd_x, odd_y = lax.rem(lax.axis_index("gx"), 2), lax.rem(lax.axis_index("gy"), 2)
    above = odd_y == parity_y
    start = pl.multiple_of(jnp.where(above, block_y - HALO, 0), 8)
    near_start = pl.multiple_of(jnp.where(above, block_y - HALF, 0), 8)
    copies = []
    for e, block in enumerate((first, second)):
        high = odd_x == e
        copies.append(
            pltpu.make_async_copy(
                block.at[:, pl.ds(jnp.where(high, 0, block_x - near), near), pl.ds(start, HALO)],
                out.at[e, :, pl.ds(0, near)],
                sems.at[2 * e],
            )
        )
        for k in range(2):
            first_plane = jnp.where(high, near, block_x - near - far) + k * (far // 2)
            copies.append(
                pltpu.make_async_copy(
                    block.at[:, pl.ds(first_plane, far // 2), pl.ds(near_start, HALF)],
                    out.at[e, :, pl.ds(near, far // 2), pl.ds(k * HALF, HALF)],
                    sems.at[4 + 2 * e + k],
                )
            )
    for copy in copies:
        copy.start()
    for copy in copies:
        copy.wait()


def pack_corners(parity_y, reach, blocks):
    shots, _, block_y, depth = blocks[0].shape
    near, far = reach
    return pl.pallas_call(
        functools.partial(corner_kernel, block_y, parity_y, reach),
        out_shape=jax.ShapeDtypeStruct((2, shots, near + far // 2, HALO, depth), jnp.float32),
        in_specs=[ANY, ANY],
        out_specs=VMEM,
        scratch_shapes=[pltpu.SemaphoreType.DMA((8,))],
        compiler_params=pltpu.CompilerParams(vmem_limit_bytes=SMALL),
        name="pack_corners",
    )(*blocks)


def side_kernel(block_y, parity_y, now, prev, out, sems):
    above = lax.rem(lax.axis_index("gy"), 2) == parity_y
    start = pl.multiple_of(jnp.where(above, block_y - HALO, 0), 8)
    copies = [
        pltpu.make_async_copy(block.at[:, :, pl.ds(start, HALO)], out.at[k], sems.at[k])
        for k, block in enumerate((now, prev))
    ]
    for copy in copies:
        copy.start()
    for copy in copies:
        copy.wait()


def pack_sides(parity_y, now, prev):
    shots, block_x, block_y, depth = now.shape
    return pl.pallas_call(
        functools.partial(side_kernel, block_y, parity_y),
        out_shape=jax.ShapeDtypeStruct((2, shots, block_x, HALO, depth), jnp.float32),
        in_specs=[ANY, ANY],
        out_specs=VMEM,
        scratch_shapes=[pltpu.SemaphoreType.DMA((2,))],
        compiler_params=pltpu.CompilerParams(vmem_limit_bytes=SMALL),
        name="pack_sides",
    )(now, prev)


def layout(sizes):
    block_x, block_y, _, _, ny = sizes
    odd_x, odd_y = lax.rem(lax.axis_index("gx"), 2), lax.rem(lax.axis_index("gy"), 2)
    own = pl.multiple_of(PAD + (HALO * odd_y if ny == 2 else HALO), 8)
    high_x = [odd_x == 0, odd_x == 1]
    high_y = [odd_y == 0, odd_y == 1]
    x_at = [jnp.where(h, HALO + block_x, 0) for h in high_x]
    y_at = [pl.multiple_of(jnp.where(h, own + block_y, own - HALO), 8) for h in high_y]
    near_y = [pl.multiple_of(jnp.where(h, own + block_y, own - HALF), 8) for h in high_y]
    return own, odd_y, high_x, x_at, y_at, near_y


def depth_in(cell, total, width):
    inside = (cell >= 0) & (cell < total)
    depth = jnp.maximum(width - jnp.minimum(cell + 1, total - cell), 0)
    return inside, depth.astype(jnp.float32) / width


def assemble_kernel(sizes, now, prev, now_x, prev_x, sides, corners_now, corners_prev, ext_all, sems):
    block_x, block_y, total_x, total_y, ny = sizes
    shots = now.shape[0]
    planes, rows, depth = ext_all.shape[1:]
    now_ext, prev_ext = ext_all.at[pl.ds(0, shots)], ext_all.at[pl.ds(shots, shots)]
    twice = ext_all.at[2 * shots + 1]
    own, _, high_x, x_at, y_at, near_y = layout(sizes)
    blank = jnp.zeros((PAD, depth), jnp.float32)

    def clear(x, _):
        for s in range(2 * shots):
            ext_all[s, x, pl.ds(0, PAD)] = blank
            ext_all[s, x, pl.ds(rows - PAD, PAD)] = blank
        return 0

    lax.fori_loop(0, planes, clear, 0)
    for f in range(len(sides)):
        for e in range(2):

            def clear_corner(x, _):
                for s in range(2 * shots):
                    for k in range(HALO // PAD):
                        ext_all[s, x_at[e] + x, pl.ds(y_at[f] + PAD * k, PAD)] = blank
                return 0

            lax.fori_loop(0, HALO, clear_corner, 0)

    copies = []

    def fetch(src, dst):
        copy = pltpu.make_async_copy(src, dst, sems.at[len(copies)])
        copy.start()
        copies.append(copy)

    def place_corner(ext, packed, reach, e, f):
        near, far = reach
        lead = pl.ds(jnp.where(high_x[e], HALO + block_x, HALO - near), near)
        fetch(packed.at[:, pl.ds(0, near)], ext.at[:, lead, pl.ds(y_at[f], HALO)])
        for k in range(2):
            first_plane = jnp.where(high_x[e], HALO + block_x + near, HALO - near - far)
            fetch(
                packed.at[:, pl.ds(near, far // 2), pl.ds(k * HALF, HALF)],
                ext.at[:, pl.ds(first_plane + k * (far // 2), far // 2), pl.ds(near_y[f], HALF)],
            )

    own_rows = pl.ds(own, block_y)
    fetch(now, now_ext.at[:, pl.ds(HALO, block_x), own_rows])
    fetch(prev, prev_ext.at[:, pl.ds(HALO, block_x), own_rows])
    for e in range(2):
        at = pl.ds(x_at[e], block_x)
        fetch(now_x[e], now_ext.at[:, at, own_rows])
        fetch(prev_x[e], prev_ext.at[:, at, own_rows])
    for f in range(len(sides)):
        at = pl.ds(y_at[f], HALO)
        fetch(sides[f].at[0], now_ext.at[:, pl.ds(HALO, block_x), at])
        fetch(sides[f].at[1], prev_ext.at[:, pl.ds(HALO, block_x), at])
        for e in range(2):
            for ext, packed, reach in (
                (now_ext, corners_now, REACH_NOW),
                (prev_ext, corners_prev, REACH_PREV),
            ):
                place_corner(ext, packed[f].at[e], reach, e, f)

    x_first = lax.axis_index("gx") * block_x - HALO
    y_first = lax.axis_index("gy") * block_y - own
    shape = (rows, depth)
    y_in, y_depth = depth_in(lax.broadcasted_iota(jnp.int32, shape, 0) + y_first, total_y, block_x)
    y_part = y_depth * y_depth

    def weigh(x, _):
        x_in, x_depth = depth_in(jnp.full(shape, x + x_first, jnp.int32), total_x, block_x)
        twice[x] = jnp.where(
            x_in & y_in, 2.0 / (1.0 + damp_peak * (x_depth * x_depth + y_part)), 0.0
        )
        return 0

    lax.fori_loop(2, planes - 2, weigh, 0)
    for copy in copies:
        copy.wait()


def call_with_groups(kernel, sizes, counts):
    def called(*refs):
        groups = []
        for count in counts:
            groups.append(refs[0] if count is None else refs[:count])
            refs = refs[1 if count is None else count:]
        kernel(sizes, *groups, *refs)

    return called


def assemble(sizes, now, prev, now_x, prev_x, sides, corners):
    block_x, block_y, _, _, ny = sizes
    shots, _, _, depth = now.shape
    planes = block_x + 2 * HALO
    rows = block_y + (HALO if ny == 2 else 2 * HALO) + 2 * PAD
    count = len(sides)
    parts = [now, prev, *now_x, *prev_x, *sides, *corners[0], *corners[1]]
    return pl.pallas_call(
        call_with_groups(assemble_kernel, sizes, (None, None, 2, 2, count, count, count)),
        out_shape=pltpu.VMEM((2 * shots + 2, planes, rows, depth), jnp.float32),
        in_specs=[ANY] * len(parts),
        out_specs=VMEM,
        scratch_shapes=[pltpu.SemaphoreType.DMA((64,))],
        compiler_params=pltpu.CompilerParams(vmem_limit_bytes=SMALL),
        name="assemble_fields",
    )(*parts)


def window_kernel(
    sizes,
    sources,
    amplitudes,
    local_list,
    _,
    speed,
    speed_x,
    speed_y,
    speed_xy,
    out_now,
    out_prev,
    partial,
    ext_all,
    samples,
    sems,
    out_sems,
):
    block_x, block_y, total_x, total_y, ny = sizes
    shots = (ext_all.shape[0] - 2) // 2
    now_ext, prev_ext = ext_all.at[pl.ds(0, shots)], ext_all.at[pl.ds(shots, shots)]
    near, twice = ext_all.at[2 * shots], ext_all.at[2 * shots + 1]
    planes, rows = ext_all.shape[1:3]
    own, odd_y, high_x, x_at, y_at, near_y = layout(sizes)
    own_rows = pl.ds(own, block_y)
    x_first = lax.axis_index("gx") * block_x - HALO
    y_first = lax.axis_index("gy") * block_y - own
    copies = []

    def fetch(src, dst):
        copy = pltpu.make_async_copy(src, dst, sems.at[len(copies)])
        copy.start()
        copies.append(copy)

    fetch(speed, near.at[pl.ds(HALO, block_x), own_rows])
    for e in range(2):
        fetch(speed_x[e], near.at[pl.ds(x_at[e], block_x), own_rows])
    for f in range(len(speed_y)):
        at = pl.ds(y_at[f], HALO)
        fetch(speed_y[f], near.at[pl.ds(HALO, block_x), at])
        for e in range(2):
            fetch(speed_xy[2 * f + e], near.at[pl.ds(x_at[e], block_x), at])
    for k in range(shots * STEPS):
        samples[k] = jnp.zeros(samples.shape[1:], jnp.float32)
    for copy in copies:
        copy.wait()

    def prepare(x, _):
        at = pl.ds(PAD, rows - 2 * PAD)
        v = near[x, at]
        near[x, at] = (0.5 * near_weight) * twice[x, at] * (v * v)
        return 0

    lax.fori_loop(2, planes - 2, prepare, 0, unroll=2)

    depth = now_ext.shape[3]
    gap = lax.broadcasted_iota(jnp.int32, (depth, depth), 0) - lax.broadcasted_iota(jnp.int32, (depth, depth), 1)
    gap = jnp.abs(gap)
    band = jnp.where(gap == 0, centre_part, jnp.where(gap == 1, 1.0, jnp.where(gap == 2, far_part, 0.0)))
    band = band.astype(jnp.bfloat16)
    band = jnp.concatenate([band, band], axis=0)
    lane_row = lax.broadcasted_iota(jnp.int32, (1, depth), 1)

    cur, old = now_ext, prev_ext
    for step in range(1, STEPS + 1):
        reach = 2 * (STEPS - step)
        side = -(-reach // 8)
        if ny == 2:
            first = pl.multiple_of(own - 8 * side * odd_y, 8)
            tiles = block_y // 8 + side
        else:
            first = pl.multiple_of(own - 8 * side, 8)
            tiles = block_y // 8 + 2 * side

        size = 8 * tiles

        def plane(g, _, cur=cur, old=old, first=first, tiles=tiles, step=step):
            x = 2 * step + GROUP * g
            for j0 in range(0, tiles, 3):
                sub = min(3, tiles - j0)
                size = 8 * sub
                start = pl.multiple_of(first + 8 * j0, 8)
                along = []
                for s in range(shots):
                    c = cur[s, pl.ds(x, GROUP), pl.ds(start, size)].reshape(GROUP * size, depth)
                    head = c.astype(jnp.bfloat16)
                    rest = (c - head.astype(jnp.float32)).astype(jnp.bfloat16)
                    parts = jnp.concatenate([head, rest], axis=1)
                    out = jnp.dot(parts, band, preferred_element_type=jnp.float32)
                    along.append(out.reshape(GROUP, size, depth))
                for j in range(sub):
                    base = start + 8 * j
                    at = pl.ds(pl.multiple_of(base, 8), 8)
                    n = [near[x + i, at] for i in range(GROUP)]
                    a = [twice[x + i, at] for i in range(GROUP)]
                    for s in range(shots):
                        c = [cur[s, x + i - 2, at] for i in range(GROUP + 4)]
                        out = []
                        for i in range(GROUP):
                            m = c[i + 2]
                            close = (c[i + 1] + c[i + 3]) + (cur[s, x + i, pl.ds(base - 1, 8)] + cur[s, x + i, pl.ds(base + 1, 8)])
                            wide = (c[i] + c[i + 4]) + (cur[s, x + i, pl.ds(base - 2, 8)] + cur[s, x + i, pl.ds(base + 2, 8)])
                            p = old[s, x + i, at]
                            lap = along[s][i, 8 * j : 8 * j + 8] + close + far_part * wide
                            out.append(p + a[i] * (m - p) + n[i] * lap)
                        for i in range(GROUP):
                            old[s, x + i, at] = out[i]
            return 0

        count = (planes - 4 * step) // GROUP
        edge = 2 if side == 2 else 0
        if edge:
            cut = functools.partial(
                plane,
                first=pl.multiple_of(own - 8 * (odd_y if ny == 2 else 1), 8),
                tiles=tiles - (1 if ny == 2 else 2),
            )
            lax.fori_loop(0, edge, cut, 0)
            lax.fori_loop(count - edge, count, cut, 0)
        lax.fori_loop(edge, count - edge, plane, 0)

        for s in range(shots):
            sx = sources[s, 0] - x_first
            sy = sources[s, 1] - y_first
            sz = sources[s, 2]
            amplitude = amplitudes[s, step - 1]
            inside = (
                (sx >= 2 * step)
                & (sx < planes - 2 * step)
                & (sy >= first)
                & (sy < first + 8 * tiles)
            )

            @pl.when(inside)
            def _(old=old, s=s, sx=sx, sy=sy, sz=sz, amplitude=amplitude):
                at = pl.ds(sy, 1)
                old[s, sx, at] += jnp.where(lane_row == sz, (0.5 * amplitude) * twice[sx, at], 0.0)

        cur, old = old, cur

        def take(g, _, cur=cur, step=step):
            found = []
            for i in range(BATCH):
                at = 1 + 3 * (BATCH * g + i)
                cell, z = local_list[at + 1], local_list[at + 2]
                x = HALO + cell // block_y
                y = own + cell % block_y
                for s in range(shots):
                    found.append(jnp.where(lane_row == z, cur[s, x, pl.ds(y, 1)], 0.0))
            for i in range(BATCH):
                r = local_list[1 + 3 * (BATCH * g + i)]
                for s in range(shots):
                    samples[s * STEPS + step - 1, pl.ds(r, 1)] = found[i * shots + s]
            return 0

        lax.fori_loop(0, (local_list[0] + BATCH - 1) // BATCH, take, 0)
        if step >= STEPS - 1:
            out = out_prev if step == STEPS - 1 else out_now
            copy = pltpu.make_async_copy(
                cur.at[:, pl.ds(HALO, block_x), own_rows],
                out,
                out_sems.at[step - STEPS + 1],
            )
            copy.start()
            if step == STEPS - 1:
                first_out = copy
            else:
                last_out = copy

    total = partial.shape[2]
    for k in range(shots * STEPS):
        values = jnp.sum(samples[k, pl.ds(0, total)], axis=1)
        for copy_to in range(partial.shape[0]):
            partial[copy_to, k] = values
    first_out.wait()
    last_out.wait()


def window(sizes, sources, amplitudes, local_list, recs, ext_all, speed, speed_x, speed_y, speed_xy, copies):
    block_x, block_y, _, _, _ = sizes
    shots = (ext_all.shape[0] - 2) // 2
    depth = ext_all.shape[3]
    field = jax.ShapeDtypeStruct((shots, block_x, block_y, depth), jnp.float32)
    count = len(speed_y)
    parts = [speed, *speed_x, *speed_y, *speed_xy]
    return pl.pallas_call(
        call_with_groups(window_kernel, sizes, (None, None, None, None, None, 2, count, 2 * count)),
        out_shape=(
            field,
            field,
            jax.ShapeDtypeStruct((copies, shots * STEPS, recs), jnp.float32),
            pltpu.VMEM(ext_all.shape, jnp.float32),
        ),
        in_specs=[SMEM] * 3 + [VMEM] + [ANY] * len(parts),
        out_specs=(ANY, ANY, VMEM, VMEM),
        input_output_aliases={3: 3},
        scratch_shapes=[
            pltpu.VMEM((shots * STEPS, recs + 8, depth), jnp.float32),
            pltpu.SemaphoreType.DMA((16,)),
            pltpu.SemaphoreType.DMA((2,)),
        ],
        compiler_params=pltpu.CompilerParams(vmem_limit_bytes=16 * 2**20),
        name="wave_window",
    )(sources, amplitudes, local_list, ext_all, *parts)


def local(model_tiles, owner_map, offsets, field_now, field_prev, sources, wavelet, receivers):
    block_x, block_y, depth = model_tiles.shape
    nx, ny, groups = lax.axis_size("gx"), lax.axis_size("gy"), lax.axis_size("sy")
    row = lax.axis_index("gy")
    total_x, total_y = block_x * nx, block_y * ny
    now, prev = field_now[0], field_prev[0]
    x_perms = [pairs(nx, 0), pairs(nx, 1)]
    y_perms = [pairs(ny, f) for f in range(2 if ny > 2 else 1)]
    spread = lax.all_to_all(model_tiles, ("sy", "gx"), 0, 0, tiled=True)
    now_x = [lax.ppermute(now, "gx", perm) for perm in x_perms]
    packed = [pack_sides(f, now, prev) for f in range(len(y_perms))]
    shifts = [offsets] + [
        lax.ppermute(offsets, "sy", [(i, (i + turn) % groups) for i in range(groups)])
        for turn in range(1, groups)
    ]
    sides = [lax.ppermute(part, "gy", perm) for part, perm in zip(packed, y_perms)]
    spread, packed, shifts, later = lax.optimization_barrier((spread, packed, shifts, prev))
    other = lax.ppermute(spread, "core", [(0, 1), (1, 0)])
    prev_x = [lax.ppermute(later, "gx", perm) for perm in x_perms]
    local_list = list_receivers(block_x, block_y, receivers[0].T)

    def cut_corners(blocks, reach):
        return [pack_corners(f, reach, blocks) for f in range(len(y_perms))]

    def swap_corners(packed):
        return [lax.ppermute(part, "gy", perm) for part, perm in zip(packed, y_perms)]


    targets = groups * nx
    slice_shape = (targets, block_x // targets, block_y, depth)
    picked = pick(nx, shifts, owner_map, spread.reshape(slice_shape), other.reshape(slice_shape))
    picked, now_x, sides = lax.optimization_barrier((picked, now_x, sides))
    cut_now = cut_corners(now_x, REACH_NOW)
    corners_now = swap_corners(cut_now)
    speed = lax.all_to_all(picked.reshape(model_tiles.shape), ("sy", "gx"), 0, 0, tiled=True)
    speed, prev_x, corners_now, local_list = lax.optimization_barrier((speed, prev_x, corners_now, local_list))
    corners = (corners_now, swap_corners(cut_corners(prev_x, REACH_PREV)))
    speed_x = [lax.ppermute(speed, "gx", perm) for perm in x_perms]
    speed_y, speed_xy = [], []
    for f, perm in enumerate(y_perms):
        start = jnp.where(row % 2 == f, block_y - HALO, 0)
        part = lax.dynamic_slice_in_dim(speed, start, HALO, axis=1)
        speed_y.append(lax.ppermute(part, "gy", perm))
        speed_xy += [lax.ppermute(part, ("gx", "gy"), joint(x_perm, perm, ny)) for x_perm in x_perms]

    sizes = (block_x, block_y, total_x, total_y, ny)
    ext_all = assemble(sizes, now, prev, now_x, prev_x, sides, corners)
    out_now, out_prev, partial, _ = window(
        sizes, sources[0], wavelet[0], local_list, receivers.shape[1],
        ext_all, speed, speed_x, speed_y, speed_xy, nx * ny,
    )
    gathered = lax.all_to_all(partial, ("gx", "gy"), 0, 0, tiled=True)
    shots = now.shape[0]
    traces = jnp.sum(gathered, axis=0).reshape(shots, STEPS, -1).transpose(0, 2, 1)
    return (out_now[None], out_prev[None], traces[None])


def solution(mesh):
    shape = dict(zip(mesh.axis_names, mesh.devices.shape))
    cores = 2 if shape["shot"] % 2 == 0 else 1
    fine = Mesh(
        mesh.devices.reshape(shape["shot"] // cores, cores, shape["gx"], shape["gy"]),
        ("sy", "core", "gx", "gy"),
    )
    shot = ("sy", "core")
    field = P(shot, None, "gx", "gy", None)
    return jax.shard_map(
        local,
        mesh=fine,
        in_specs=(
            P(("sy", "core", "gx"), "gy", None),
            P(),
            P(shot),
            field,
            field,
            P(shot, None, None),
            P(shot, None, None),
            P(shot, None, None),
        ),
        out_specs=(field, field, P(shot, None, None, None)),
        check_vma=False,
    )
```

```python
import functools

import jax
import jax.numpy as jnp
from jax import lax
from jax.experimental import pallas as pl
from jax.experimental.pallas import tpu as pltpu
from jax.sharding import Mesh
from jax.sharding import PartitionSpec as P

STEPS = 8
HALO = 2 * STEPS
PAD = 8
HALF = HALO // 2
REACH_NOW = (HALF - 1, HALF)
REACH_PREV = (HALF - 3, HALF)
WIDEST = 10
BATCH = 4

near_weight = 4.0 / 3.0
centre_part = -7.5 * 0.75
far_part = -1.0 / 16.0
damp_peak = 0.3

SMEM = pl.BlockSpec(memory_space=pltpu.SMEM)
ANY = pl.BlockSpec(memory_space=pl.ANY)
SMALL = 4 * 2**20
VMEM = pl.BlockSpec(memory_space=pltpu.VMEM)


def in_hbm(array):
    return pltpu.with_memory_space_constraint(array, pltpu.HBM)


def pairs(count, parity):
    return [
        pair
        for i in range(parity, count - 1, 2)
        for pair in ((i, i + 1), (i + 1, i))
    ]


def joint(first, second, count):
    return [(a * count + b, c * count + d) for a, c in first for b, d in second]


def list_kernel(block_x, block_y, receivers, local_list):
    x_first, y_first = lax.axis_index("gx") * block_x, lax.axis_index("gy") * block_y
    total = receivers.shape[1]
    batch = 8

    def body(g, count):
        for i in range(batch):
            r = g * batch + i
            x = receivers[0, r] - x_first
            y = receivers[1, r] - y_first
            inside = (x >= 0) & (x < block_x) & (y >= 0) & (y < block_y)
            local_list[1 + 3 * count] = r
            local_list[2 + 3 * count] = x * block_y + y
            local_list[3 + 3 * count] = receivers[2, r]
            count = count + inside.astype(jnp.int32)
        return count

    count = lax.fori_loop(0, total // batch, body, jnp.int32(0))
    local_list[0] = count
    for i in range(BATCH):
        local_list[1 + 3 * (count + i)] = total
        local_list[2 + 3 * (count + i)] = 0
        local_list[3 + 3 * (count + i)] = 0


def list_receivers(block_x, block_y, receivers):
    total = receivers.shape[1]
    return pl.pallas_call(
        functools.partial(list_kernel, block_x, block_y),
        out_shape=jax.ShapeDtypeStruct((3 * (total + BATCH) + 8,), jnp.int32),
        in_specs=[SMEM],
        out_specs=SMEM,
        compiler_params=pltpu.CompilerParams(vmem_limit_bytes=SMALL),
        name="list_receivers",
    )(receivers)


def pick_kernel(across, groups, owner_map, *refs):
    shifts, (stored, other, out, sems) = refs[:groups], refs[groups:]
    core, mine = lax.axis_index("core"), lax.axis_index("sy")
    copies = []
    for turn in range(groups):
        group = lax.rem(mine + groups - turn, groups)
        for z in range(across):
            block = owner_map[shifts[turn][0] + z]
            owner_core = lax.rem(block // across, 2)
            row = (block // (2 * across)) * across + lax.rem(block, across)
            t = group * across + z
            here = pltpu.make_async_copy(stored.at[row], out.at[t], sems.at[len(copies)])
            there = pltpu.make_async_copy(other.at[row], out.at[t], sems.at[len(copies)])
            pl.when(owner_core == core)(here.start)
            pl.when(owner_core != core)(there.start)
            copies.append(here)
    for copy in copies:
        copy.wait()


def pick(across, shifts, owner_map, stored, other):
    targets = stored.shape[0]
    return pl.pallas_call(
        functools.partial(pick_kernel, across, len(shifts)),
        out_shape=jax.ShapeDtypeStruct(stored.shape, stored.dtype),
        in_specs=[SMEM] * (1 + len(shifts)) + [ANY, ANY],
        out_specs=VMEM,
        scratch_shapes=[pltpu.SemaphoreType.DMA((targets,))],
        compiler_params=pltpu.CompilerParams(vmem_limit_bytes=SMALL),
        name="pick_slices",
    )(owner_map, *shifts, stored, other)


def corner_kernel(block_y, parity_y, reach, first, second, out, sems):
    near, far = reach
    block_x = first.shape[1]
    odd_x, odd_y = lax.rem(lax.axis_index("gx"), 2), lax.rem(lax.axis_index("gy"), 2)
    above = odd_y == parity_y
    start = pl.multiple_of(jnp.where(above, block_y - HALO, 0), 8)
    near_start = pl.multiple_of(jnp.where(above, block_y - HALF, 0), 8)
    copies = []
    for e, block in enumerate((first, second)):
        high = odd_x == e
        copies.append(
            pltpu.make_async_copy(
                block.at[:, pl.ds(jnp.where(high, 0, block_x - near), near), pl.ds(start, HALO)],
                out.at[e, :, pl.ds(0, near)],
                sems.at[2 * e],
            )
        )
        for k in range(2):
            first_plane = jnp.where(high, near, block_x - near - far) + k * (far // 2)
            copies.append(
                pltpu.make_async_copy(
                    block.at[:, pl.ds(first_plane, far // 2), pl.ds(near_start, HALF)],
                    out.at[e, :, pl.ds(near, far // 2), pl.ds(k * HALF, HALF)],
                    sems.at[4 + 2 * e + k],
                )
            )
    for copy in copies:
        copy.start()
    for copy in copies:
        copy.wait()


def pack_corners(parity_y, reach, blocks):
    shots, _, block_y, depth = blocks[0].shape
    near, far = reach
    return pl.pallas_call(
        functools.partial(corner_kernel, block_y, parity_y, reach),
        out_shape=jax.ShapeDtypeStruct((2, shots, near + far // 2, HALO, depth), jnp.float32),
        in_specs=[ANY, ANY],
        out_specs=VMEM,
        scratch_shapes=[pltpu.SemaphoreType.DMA((8,))],
        compiler_params=pltpu.CompilerParams(vmem_limit_bytes=SMALL),
        name="pack_corners",
    )(*blocks)


def side_kernel(block_y, parity_y, now, prev, out, sems):
    above = lax.rem(lax.axis_index("gy"), 2) == parity_y
    start = pl.multiple_of(jnp.where(above, block_y - HALO, 0), 8)
    copies = [
        pltpu.make_async_copy(block.at[:, :, pl.ds(start, HALO)], out.at[k], sems.at[k])
        for k, block in enumerate((now, prev))
    ]
    for copy in copies:
        copy.start()
    for copy in copies:
        copy.wait()


def pack_sides(parity_y, now, prev):
    shots, block_x, block_y, depth = now.shape
    now, prev = in_hbm(now), in_hbm(prev)
    return pl.pallas_call(
        functools.partial(side_kernel, block_y, parity_y),
        out_shape=jax.ShapeDtypeStruct((2, shots, block_x, HALO, depth), jnp.float32),
        in_specs=[ANY, ANY],
        out_specs=VMEM,
        scratch_shapes=[pltpu.SemaphoreType.DMA((2,))],
        compiler_params=pltpu.CompilerParams(vmem_limit_bytes=SMALL),
        name="pack_sides",
    )(now, prev)


def layout(sizes):
    block_x, block_y, _, _, ny = sizes
    odd_x, odd_y = lax.rem(lax.axis_index("gx"), 2), lax.rem(lax.axis_index("gy"), 2)
    own = pl.multiple_of(PAD + (HALO * odd_y if ny == 2 else HALO), 8)
    high_x = [odd_x == 0, odd_x == 1]
    high_y = [odd_y == 0, odd_y == 1]
    x_at = [jnp.where(h, HALO + block_x, 0) for h in high_x]
    y_at = [pl.multiple_of(jnp.where(h, own + block_y, own - HALO), 8) for h in high_y]
    near_y = [pl.multiple_of(jnp.where(h, own + block_y, own - HALF), 8) for h in high_y]
    return own, odd_y, high_x, x_at, y_at, near_y


def depth_in(cell, total, width):
    inside = (cell >= 0) & (cell < total)
    depth = jnp.maximum(width - jnp.minimum(cell + 1, total - cell), 0)
    return inside, depth.astype(jnp.float32) / width


def assemble_kernel(sizes, now, prev, now_x, prev_x, sides, corners_now, corners_prev, ext_all, sems):
    block_x, block_y, total_x, total_y, ny = sizes
    shots = now.shape[0]
    planes, rows, depth = ext_all.shape[1:]
    now_ext, prev_ext = ext_all.at[pl.ds(0, shots)], ext_all.at[pl.ds(shots, shots)]
    twice = ext_all.at[2 * shots + 1]
    own, _, high_x, x_at, y_at, near_y = layout(sizes)
    blank = jnp.zeros((PAD, depth), jnp.float32)

    def clear(x, _):
        for s in range(2 * shots):
            ext_all[s, x, pl.ds(0, PAD)] = blank
            ext_all[s, x, pl.ds(rows - PAD, PAD)] = blank
        return 0

    lax.fori_loop(0, planes, clear, 0)
    for f in range(len(sides)):
        for e in range(2):

            def clear_corner(x, _):
                for s in range(2 * shots):
                    for k in range(HALO // PAD):
                        ext_all[s, x_at[e] + x, pl.ds(y_at[f] + PAD * k, PAD)] = blank
                return 0

            lax.fori_loop(0, HALO, clear_corner, 0)

    copies = []

    def fetch(src, dst):
        copy = pltpu.make_async_copy(src, dst, sems.at[len(copies)])
        copy.start()
        copies.append(copy)

    def place_corner(ext, packed, reach, e, f):
        near, far = reach
        lead = pl.ds(jnp.where(high_x[e], HALO + block_x, HALO - near), near)
        fetch(packed.at[:, pl.ds(0, near)], ext.at[:, lead, pl.ds(y_at[f], HALO)])
        for k in range(2):
            first_plane = jnp.where(high_x[e], HALO + block_x + near, HALO - near - far)
            fetch(
                packed.at[:, pl.ds(near, far // 2), pl.ds(k * HALF, HALF)],
                ext.at[:, pl.ds(first_plane + k * (far // 2), far // 2), pl.ds(near_y[f], HALF)],
            )

    own_rows = pl.ds(own, block_y)
    fetch(now, now_ext.at[:, pl.ds(HALO, block_x), own_rows])
    fetch(prev, prev_ext.at[:, pl.ds(HALO, block_x), own_rows])
    for e in range(2):
        at = pl.ds(x_at[e], block_x)
        fetch(now_x[e], now_ext.at[:, at, own_rows])
        fetch(prev_x[e], prev_ext.at[:, at, own_rows])
    for f in range(len(sides)):
        at = pl.ds(y_at[f], HALO)
        fetch(sides[f].at[0], now_ext.at[:, pl.ds(HALO, block_x), at])
        fetch(sides[f].at[1], prev_ext.at[:, pl.ds(HALO, block_x), at])
        for e in range(2):
            for ext, packed, reach in (
                (now_ext, corners_now, REACH_NOW),
                (prev_ext, corners_prev, REACH_PREV),
            ):
                place_corner(ext, packed[f].at[e], reach, e, f)

    x_first = lax.axis_index("gx") * block_x - HALO
    y_first = lax.axis_index("gy") * block_y - own
    shape = (rows, depth)
    y_in, y_depth = depth_in(lax.broadcasted_iota(jnp.int32, shape, 0) + y_first, total_y, block_x)
    y_part = y_depth * y_depth

    def weigh(x, _):
        x_in, x_depth = depth_in(jnp.full(shape, x + x_first, jnp.int32), total_x, block_x)
        twice[x] = jnp.where(
            x_in & y_in, 2.0 / (1.0 + damp_peak * (x_depth * x_depth + y_part)), 0.0
        )
        return 0

    lax.fori_loop(2, planes - 2, weigh, 0)
    for copy in copies:
        copy.wait()


def call_with_groups(kernel, sizes, counts):
    def called(*refs):
        groups = []
        for count in counts:
            groups.append(refs[0] if count is None else refs[:count])
            refs = refs[1 if count is None else count:]
        kernel(sizes, *groups, *refs)

    return called


def assemble(sizes, now, prev, now_x, prev_x, sides, corners):
    block_x, block_y, _, _, ny = sizes
    shots, _, _, depth = now.shape
    planes = block_x + 2 * HALO
    rows = block_y + (HALO if ny == 2 else 2 * HALO) + 2 * PAD
    count = len(sides)
    parts = [in_hbm(now), in_hbm(prev), *now_x, *prev_x, *sides, *corners[0], *corners[1]]
    return pl.pallas_call(
        call_with_groups(assemble_kernel, sizes, (None, None, 2, 2, count, count, count)),
        out_shape=pltpu.VMEM((2 * shots + 2, planes, rows, depth), jnp.float32),
        in_specs=[ANY] * len(parts),
        out_specs=VMEM,
        scratch_shapes=[pltpu.SemaphoreType.DMA((64,))],
        compiler_params=pltpu.CompilerParams(vmem_limit_bytes=SMALL),
        name="assemble_fields",
    )(*parts)


def window_kernel(
    sizes,
    sources,
    amplitudes,
    local_list,
    _,
    speed,
    speed_x,
    speed_y,
    speed_xy,
    out_now,
    out_prev,
    partial,
    ext_all,
    samples,
    sems,
    out_sems,
):
    block_x, block_y, total_x, total_y, ny = sizes
    shots = (ext_all.shape[0] - 2) // 2
    now_ext, prev_ext = ext_all.at[pl.ds(0, shots)], ext_all.at[pl.ds(shots, shots)]
    near, twice = ext_all.at[2 * shots], ext_all.at[2 * shots + 1]
    planes, rows = ext_all.shape[1:3]
    own, odd_y, high_x, x_at, y_at, near_y = layout(sizes)
    own_rows = pl.ds(own, block_y)
    x_first = lax.axis_index("gx") * block_x - HALO
    y_first = lax.axis_index("gy") * block_y - own
    copies = []

    def fetch(src, dst):
        copy = pltpu.make_async_copy(src, dst, sems.at[len(copies)])
        copy.start()
        copies.append(copy)

    fetch(speed, near.at[pl.ds(HALO, block_x), own_rows])
    for e in range(2):
        fetch(speed_x[e], near.at[pl.ds(x_at[e], block_x), own_rows])
    for f in range(len(speed_y)):
        at = pl.ds(y_at[f], HALO)
        fetch(speed_y[f], near.at[pl.ds(HALO, block_x), at])
        for e in range(2):
            fetch(speed_xy[2 * f + e], near.at[pl.ds(x_at[e], block_x), at])
    for k in range(shots * STEPS):
        samples[k] = jnp.zeros(samples.shape[1:], jnp.float32)
    for copy in copies:
        copy.wait()

    def prepare(x, _):
        at = pl.ds(PAD, rows - 2 * PAD)
        v = near[x, at]
        near[x, at] = (0.5 * near_weight) * twice[x, at] * (v * v)
        return 0

    lax.fori_loop(2, planes - 2, prepare, 0, unroll=2)

    depth = now_ext.shape[3]
    gap = lax.broadcasted_iota(jnp.int32, (depth, depth), 0) - lax.broadcasted_iota(jnp.int32, (depth, depth), 1)
    gap = jnp.abs(gap)
    band = jnp.where(gap == 0, centre_part, jnp.where(gap == 1, 1.0, jnp.where(gap == 2, far_part, 0.0)))
    band = band.astype(jnp.bfloat16)
    band = jnp.concatenate([band, band], axis=0)
    lane_row = lax.broadcasted_iota(jnp.int32, (1, depth), 1)

    cur, old = now_ext, prev_ext
    for step in range(1, STEPS + 1):
        reach = 2 * (STEPS - step)
        side = -(-reach // 8)
        if ny == 2:
            first = pl.multiple_of(own - 8 * side * odd_y, 8)
            tiles = block_y // 8 + side
        else:
            first = pl.multiple_of(own - 8 * side, 8)
            tiles = block_y // 8 + 2 * side

        size = 8 * tiles

        def some(g, _, at_x, size_x, first, tiles, cur=cur, old=old):
            x = at_x + size_x * g
            for j0 in range(0, tiles, 3):
                sub = min(3, tiles - j0)
                size = 8 * sub
                start = pl.multiple_of(first + 8 * j0, 8)
                along = []
                for s in range(shots):
                    c = cur[s, pl.ds(x, size_x), pl.ds(start, size)].reshape(size_x * size, depth)
                    head = c.astype(jnp.bfloat16)
                    rest = (c - head.astype(jnp.float32)).astype(jnp.bfloat16)
                    parts = jnp.concatenate([head, rest], axis=1)
                    out = jnp.dot(parts, band, preferred_element_type=jnp.float32)
                    along.append(out.reshape(size_x, size, depth))
                for j in range(sub):
                    base = start + 8 * j
                    at = pl.ds(pl.multiple_of(base, 8), 8)
                    n = [near[x + i, at] for i in range(size_x)]
                    a = [twice[x + i, at] for i in range(size_x)]
                    for s in range(shots):
                        c = [cur[s, x + i - 2, at] for i in range(size_x + 4)]
                        out = []
                        for i in range(size_x):
                            m = c[i + 2]
                            close = (c[i + 1] + c[i + 3]) + (cur[s, x + i, pl.ds(base - 1, 8)] + cur[s, x + i, pl.ds(base + 1, 8)])
                            wide = (c[i] + c[i + 4]) + (cur[s, x + i, pl.ds(base - 2, 8)] + cur[s, x + i, pl.ds(base + 2, 8)])
                            p = old[s, x + i, at]
                            lap = along[s][i, 8 * j : 8 * j + 8] + close + far_part * wide
                            out.append(p + a[i] * (m - p) + n[i] * lap)
                        for i in range(size_x):
                            old[s, x + i, at] = out[i]
            return 0

        def sweep(at_x, count, first, tiles):
            size_x = max(n for n in range(1, WIDEST + 1) if count % n == 0)
            part = functools.partial(some, at_x=at_x, size_x=size_x, first=first, tiles=tiles)
            lax.fori_loop(0, count // size_x, part, 0)

        edge = 8 if side == 2 else 0
        if edge:
            near_first = pl.multiple_of(own - 8 * (odd_y if ny == 2 else 1), 8)
            near_tiles = tiles - (1 if ny == 2 else 2)
            sweep(2 * step, edge, near_first, near_tiles)
            sweep(planes - 2 * step - edge, edge, near_first, near_tiles)
        sweep(2 * step + edge, planes - 4 * step - 2 * edge, first, tiles)

        for s in range(shots):
            sx = sources[s, 0] - x_first
            sy = sources[s, 1] - y_first
            sz = sources[s, 2]
            amplitude = amplitudes[s, step - 1]
            inside = (
                (sx >= 2 * step)
                & (sx < planes - 2 * step)
                & (sy >= first)
                & (sy < first + 8 * tiles)
            )

            @pl.when(inside)
            def _(old=old, s=s, sx=sx, sy=sy, sz=sz, amplitude=amplitude):
                at = pl.ds(sy, 1)
                old[s, sx, at] += jnp.where(lane_row == sz, (0.5 * amplitude) * twice[sx, at], 0.0)

        cur, old = old, cur

        def take(g, _, cur=cur, step=step):
            found = []
            for i in range(BATCH):
                at = 1 + 3 * (BATCH * g + i)
                cell, z = local_list[at + 1], local_list[at + 2]
                x = HALO + cell // block_y
                y = own + cell % block_y
                for s in range(shots):
                    found.append(jnp.where(lane_row == z, cur[s, x, pl.ds(y, 1)], 0.0))
            for i in range(BATCH):
                r = local_list[1 + 3 * (BATCH * g + i)]
                for s in range(shots):
                    samples[s * STEPS + step - 1, pl.ds(r, 1)] = found[i * shots + s]
            return 0

        lax.fori_loop(0, (local_list[0] + BATCH - 1) // BATCH, take, 0)
        if step >= STEPS - 1:
            out = out_prev if step == STEPS - 1 else out_now
            copy = pltpu.make_async_copy(
                cur.at[:, pl.ds(HALO, block_x), own_rows],
                out,
                out_sems.at[step - STEPS + 1],
            )
            copy.start()
            if step == STEPS - 1:
                first_out = copy
            else:
                last_out = copy

    total = partial.shape[2]
    for k in range(shots * STEPS):
        values = jnp.sum(samples[k, pl.ds(0, total)], axis=1)
        for copy_to in range(partial.shape[0]):
            partial[copy_to, k] = values
    first_out.wait()
    last_out.wait()


def window(sizes, sources, amplitudes, local_list, recs, ext_all, speed, speed_x, speed_y, speed_xy, copies):
    block_x, block_y, _, _, _ = sizes
    shots = (ext_all.shape[0] - 2) // 2
    depth = ext_all.shape[3]
    field = jax.ShapeDtypeStruct((shots, block_x, block_y, depth), jnp.float32)
    count = len(speed_y)
    parts = [speed, *speed_x, *speed_y, *speed_xy]
    return pl.pallas_call(
        call_with_groups(window_kernel, sizes, (None, None, None, None, None, 2, count, 2 * count)),
        out_shape=(
            field,
            field,
            jax.ShapeDtypeStruct((copies, shots * STEPS, recs), jnp.float32),
            pltpu.VMEM(ext_all.shape, jnp.float32),
        ),
        in_specs=[SMEM] * 3 + [VMEM] + [ANY] * len(parts),
        out_specs=(ANY, ANY, VMEM, VMEM),
        input_output_aliases={3: 3},
        scratch_shapes=[
            pltpu.VMEM((shots * STEPS, recs + 8, depth), jnp.float32),
            pltpu.SemaphoreType.DMA((16,)),
            pltpu.SemaphoreType.DMA((2,)),
        ],
        compiler_params=pltpu.CompilerParams(vmem_limit_bytes=16 * 2**20),
        name="wave_window",
    )(sources, amplitudes, local_list, ext_all, *parts)


def local(model_tiles, owner_map, offsets, field_now, field_prev, sources, wavelet, receivers):
    block_x, block_y, depth = model_tiles.shape
    nx, ny, groups = lax.axis_size("gx"), lax.axis_size("gy"), lax.axis_size("sy")
    row = lax.axis_index("gy")
    total_x, total_y = block_x * nx, block_y * ny
    now, prev = field_now[0], field_prev[0]
    x_perms = [pairs(nx, 0), pairs(nx, 1)]
    y_perms = [pairs(ny, f) for f in range(2 if ny > 2 else 1)]
    spread = lax.all_to_all(model_tiles, ("sy", "gx"), 0, 0, tiled=True)
    now_x = [lax.ppermute(now, "gx", perm) for perm in x_perms]
    packed = [pack_sides(f, now, prev) for f in range(len(y_perms))]
    shifts = [offsets] + [
        lax.ppermute(offsets, "sy", [(i, (i + turn) % groups) for i in range(groups)])
        for turn in range(1, groups)
    ]
    sides = [lax.ppermute(part, "gy", perm) for part, perm in zip(packed, y_perms)]
    spread, packed, shifts, later = lax.optimization_barrier((spread, packed, shifts, prev))
    other = lax.ppermute(spread, "core", [(0, 1), (1, 0)])
    prev_x = [lax.ppermute(later, "gx", perm) for perm in x_perms]
    local_list = list_receivers(block_x, block_y, receivers[0].T)

    def cut_corners(blocks, reach):
        return [pack_corners(f, reach, blocks) for f in range(len(y_perms))]

    def swap_corners(packed):
        return [lax.ppermute(part, "gy", perm) for part, perm in zip(packed, y_perms)]


    targets = groups * nx
    slice_shape = (targets, block_x // targets, block_y, depth)
    picked = pick(nx, shifts, owner_map, spread.reshape(slice_shape), other.reshape(slice_shape))
    picked, now_x, sides = lax.optimization_barrier((picked, now_x, sides))
    cut_now = cut_corners(now_x, REACH_NOW)
    corners_now = swap_corners(cut_now)
    speed = lax.all_to_all(picked.reshape(model_tiles.shape), ("sy", "gx"), 0, 0, tiled=True)
    speed, prev_x, corners_now, local_list = lax.optimization_barrier((speed, prev_x, corners_now, local_list))
    corners = (corners_now, swap_corners(cut_corners(prev_x, REACH_PREV)))
    speed_x = [lax.ppermute(speed, "gx", perm) for perm in x_perms]
    speed_y, speed_xy = [], []
    for f, perm in enumerate(y_perms):
        start = jnp.where(row % 2 == f, block_y - HALO, 0)
        part = lax.dynamic_slice_in_dim(speed, start, HALO, axis=1)
        speed_y.append(lax.ppermute(part, "gy", perm))
        speed_xy += [lax.ppermute(part, ("gx", "gy"), joint(x_perm, perm, ny)) for x_perm in x_perms]

    sizes = (block_x, block_y, total_x, total_y, ny)
    ext_all = assemble(sizes, now, prev, now_x, prev_x, sides, corners)
    out_now, out_prev, partial, _ = window(
        sizes, sources[0], wavelet[0], local_list, receivers.shape[1],
        ext_all, speed, speed_x, speed_y, speed_xy, nx * ny,
    )
    gathered = lax.all_to_all(partial, ("gx", "gy"), 0, 0, tiled=True)
    shots = now.shape[0]
    traces = jnp.sum(gathered, axis=0).reshape(shots, STEPS, -1).transpose(0, 2, 1)
    return (out_now[None], out_prev[None], traces[None])


def solution(mesh):
    shape = dict(zip(mesh.axis_names, mesh.devices.shape))
    cores = 2 if shape["shot"] % 2 == 0 else 1
    fine = Mesh(
        mesh.devices.reshape(shape["shot"] // cores, cores, shape["gx"], shape["gy"]),
        ("sy", "core", "gx", "gy"),
    )
    shot = ("sy", "core")
    field = P(shot, None, "gx", "gy", None)
    return jax.shard_map(
        local,
        mesh=fine,
        in_specs=(
            P(("sy", "core", "gx"), "gy", None),
            P(),
            P(shot),
            field,
            field,
            P(shot, None, None),
            P(shot, None, None),
            P(shot, None, None),
        ),
        out_specs=(field, field, P(shot, None, None, None)),
        check_vma=False,
    )
```

```python
import functools

import jax
import jax.numpy as jnp
from jax import lax
from jax.experimental import pallas as pl
from jax.experimental.pallas import tpu as pltpu
from jax.sharding import Mesh
from jax.sharding import PartitionSpec as P

STEPS = 8
HALO = 2 * STEPS
PAD = 8
HALF = HALO // 2
REACH_NOW = (HALF - 1, HALF)
REACH_PREV = (HALF - 3, HALF)
WIDEST = 10
BATCH = 4

near_weight = 4.0 / 3.0
centre_part = -7.5 * 0.75
far_part = -1.0 / 16.0
damp_peak = 0.3

SMEM = pl.BlockSpec(memory_space=pltpu.SMEM)
ANY = pl.BlockSpec(memory_space=pl.ANY)
SMALL = 4 * 2**20
VMEM = pl.BlockSpec(memory_space=pltpu.VMEM)


def in_hbm(array):
    return pltpu.with_memory_space_constraint(array, pltpu.HBM)


def pairs(count, parity):
    return [
        pair
        for i in range(parity, count - 1, 2)
        for pair in ((i, i + 1), (i + 1, i))
    ]


def joint(first, second, count):
    return [(a * count + b, c * count + d) for a, c in first for b, d in second]


def list_kernel(block_x, block_y, receivers, local_list):
    x_first, y_first = lax.axis_index("gx") * block_x, lax.axis_index("gy") * block_y
    total = receivers.shape[1]
    batch = 8

    def body(g, count):
        for i in range(batch):
            r = g * batch + i
            x = receivers[0, r] - x_first
            y = receivers[1, r] - y_first
            inside = (x >= 0) & (x < block_x) & (y >= 0) & (y < block_y)
            local_list[1 + 3 * count] = r
            local_list[2 + 3 * count] = x * block_y + y
            local_list[3 + 3 * count] = receivers[2, r]
            count = count + inside.astype(jnp.int32)
        return count

    count = lax.fori_loop(0, total // batch, body, jnp.int32(0))
    local_list[0] = count
    for i in range(BATCH):
        local_list[1 + 3 * (count + i)] = total
        local_list[2 + 3 * (count + i)] = 0
        local_list[3 + 3 * (count + i)] = 0


def list_receivers(block_x, block_y, receivers):
    total = receivers.shape[1]
    return pl.pallas_call(
        functools.partial(list_kernel, block_x, block_y),
        out_shape=jax.ShapeDtypeStruct((3 * (total + BATCH) + 8,), jnp.int32),
        in_specs=[SMEM],
        out_specs=SMEM,
        compiler_params=pltpu.CompilerParams(vmem_limit_bytes=SMALL),
        name="list_receivers",
    )(receivers)


def pick_kernel(across, groups, owner_map, *refs):
    shifts, (stored, other, out, sems) = refs[:groups], refs[groups:]
    core, mine = lax.axis_index("core"), lax.axis_index("sy")
    copies = []
    for turn in range(groups):
        group = lax.rem(mine + groups - turn, groups)
        for z in range(across):
            block = owner_map[shifts[turn][0] + z]
            owner_core = lax.rem(block // across, 2)
            row = (block // (2 * across)) * across + lax.rem(block, across)
            t = group * across + z
            here = pltpu.make_async_copy(stored.at[row], out.at[t], sems.at[len(copies)])
            there = pltpu.make_async_copy(other.at[row], out.at[t], sems.at[len(copies)])
            pl.when(owner_core == core)(here.start)
            pl.when(owner_core != core)(there.start)
            copies.append(here)
    for copy in copies:
        copy.wait()


def pick(across, shifts, owner_map, stored, other):
    targets = stored.shape[0]
    return pl.pallas_call(
        functools.partial(pick_kernel, across, len(shifts)),
        out_shape=jax.ShapeDtypeStruct(stored.shape, stored.dtype),
        in_specs=[SMEM] * (1 + len(shifts)) + [ANY, ANY],
        out_specs=VMEM,
        scratch_shapes=[pltpu.SemaphoreType.DMA((targets,))],
        compiler_params=pltpu.CompilerParams(vmem_limit_bytes=SMALL),
        name="pick_slices",
    )(owner_map, *shifts, stored, other)


def corner_kernel(block_y, parity_y, reach, first, second, out, sems):
    near, far = reach
    block_x = first.shape[1]
    odd_x, odd_y = lax.rem(lax.axis_index("gx"), 2), lax.rem(lax.axis_index("gy"), 2)
    above = odd_y == parity_y
    start = pl.multiple_of(jnp.where(above, block_y - HALO, 0), 8)
    near_start = pl.multiple_of(jnp.where(above, block_y - HALF, 0), 8)
    copies = []
    for e, block in enumerate((first, second)):
        high = odd_x == e
        copies.append(
            pltpu.make_async_copy(
                block.at[:, pl.ds(jnp.where(high, 0, block_x - near), near), pl.ds(start, HALO)],
                out.at[e, :, pl.ds(0, near)],
                sems.at[2 * e],
            )
        )
        for k in range(2):
            first_plane = jnp.where(high, near, block_x - near - far) + k * (far // 2)
            copies.append(
                pltpu.make_async_copy(
                    block.at[:, pl.ds(first_plane, far // 2), pl.ds(near_start, HALF)],
                    out.at[e, :, pl.ds(near, far // 2), pl.ds(k * HALF, HALF)],
                    sems.at[4 + 2 * e + k],
                )
            )
    for copy in copies:
        copy.start()
    for copy in copies:
        copy.wait()


def pack_corners(parity_y, reach, blocks):
    shots, _, block_y, depth = blocks[0].shape
    near, far = reach
    return pl.pallas_call(
        functools.partial(corner_kernel, block_y, parity_y, reach),
        out_shape=jax.ShapeDtypeStruct((2, shots, near + far // 2, HALO, depth), jnp.float32),
        in_specs=[ANY, ANY],
        out_specs=VMEM,
        scratch_shapes=[pltpu.SemaphoreType.DMA((8,))],
        compiler_params=pltpu.CompilerParams(vmem_limit_bytes=SMALL),
        name="pack_corners",
    )(*blocks)


def side_kernel(block_y, parity_y, now, prev, out, sems):
    above = lax.rem(lax.axis_index("gy"), 2) == parity_y
    start = pl.multiple_of(jnp.where(above, block_y - HALO, 0), 8)
    copies = [
        pltpu.make_async_copy(block.at[:, :, pl.ds(start, HALO)], out.at[k], sems.at[k])
        for k, block in enumerate((now, prev))
    ]
    for copy in copies:
        copy.start()
    for copy in copies:
        copy.wait()


def pack_sides(parity_y, now, prev):
    shots, block_x, block_y, depth = now.shape
    now, prev = in_hbm(now), in_hbm(prev)
    return pl.pallas_call(
        functools.partial(side_kernel, block_y, parity_y),
        out_shape=jax.ShapeDtypeStruct((2, shots, block_x, HALO, depth), jnp.float32),
        in_specs=[ANY, ANY],
        out_specs=VMEM,
        scratch_shapes=[pltpu.SemaphoreType.DMA((2,))],
        compiler_params=pltpu.CompilerParams(vmem_limit_bytes=SMALL),
        name="pack_sides",
    )(now, prev)


def layout(sizes):
    block_x, block_y, _, _, ny = sizes
    odd_x, odd_y = lax.rem(lax.axis_index("gx"), 2), lax.rem(lax.axis_index("gy"), 2)
    own = pl.multiple_of(PAD + (HALO * odd_y if ny == 2 else HALO), 8)
    high_x = [odd_x == 0, odd_x == 1]
    high_y = [odd_y == 0, odd_y == 1]
    x_at = [jnp.where(h, HALO + block_x, 0) for h in high_x]
    y_at = [pl.multiple_of(jnp.where(h, own + block_y, own - HALO), 8) for h in high_y]
    near_y = [pl.multiple_of(jnp.where(h, own + block_y, own - HALF), 8) for h in high_y]
    return own, odd_y, high_x, x_at, y_at, near_y


def depth_in(cell, total, width):
    inside = (cell >= 0) & (cell < total)
    depth = jnp.maximum(width - jnp.minimum(cell + 1, total - cell), 0)
    return inside, depth.astype(jnp.float32) / width


def assemble_kernel(sizes, now, prev, now_x, prev_x, sides, corners_now, corners_prev, ext_all, sems):
    block_x, block_y, total_x, total_y, ny = sizes
    shots = now.shape[0]
    planes, rows, depth = ext_all.shape[1:]
    now_ext, prev_ext = ext_all.at[pl.ds(0, shots)], ext_all.at[pl.ds(shots, shots)]
    twice = ext_all.at[2 * shots + 1]
    own, _, high_x, x_at, y_at, near_y = layout(sizes)
    blank = jnp.zeros((PAD, depth), jnp.float32)

    def clear(x, _):
        for s in range(2 * shots):
            ext_all[s, x, pl.ds(0, PAD)] = blank
            ext_all[s, x, pl.ds(rows - PAD, PAD)] = blank
        return 0

    lax.fori_loop(0, planes, clear, 0)
    for f in range(len(sides)):
        for e in range(2):

            def clear_corner(x, _):
                for s in range(2 * shots):
                    for k in range(HALO // PAD):
                        ext_all[s, x_at[e] + x, pl.ds(y_at[f] + PAD * k, PAD)] = blank
                return 0

            lax.fori_loop(0, HALO, clear_corner, 0)

    copies = []

    def fetch(src, dst):
        copy = pltpu.make_async_copy(src, dst, sems.at[len(copies)])
        copy.start()
        copies.append(copy)

    def place_corner(ext, packed, reach, e, f):
        near, far = reach
        lead = pl.ds(jnp.where(high_x[e], HALO + block_x, HALO - near), near)
        fetch(packed.at[:, pl.ds(0, near)], ext.at[:, lead, pl.ds(y_at[f], HALO)])
        for k in range(2):
            first_plane = jnp.where(high_x[e], HALO + block_x + near, HALO - near - far)
            fetch(
                packed.at[:, pl.ds(near, far // 2), pl.ds(k * HALF, HALF)],
                ext.at[:, pl.ds(first_plane + k * (far // 2), far // 2), pl.ds(near_y[f], HALF)],
            )

    own_rows = pl.ds(own, block_y)
    fetch(now, now_ext.at[:, pl.ds(HALO, block_x), own_rows])
    fetch(prev, prev_ext.at[:, pl.ds(HALO, block_x), own_rows])
    for e in range(2):
        at = pl.ds(x_at[e], block_x)
        fetch(now_x[e], now_ext.at[:, at, own_rows])
        fetch(prev_x[e], prev_ext.at[:, at, own_rows])
    for f in range(len(sides)):
        at = pl.ds(y_at[f], HALO)
        fetch(sides[f].at[0], now_ext.at[:, pl.ds(HALO, block_x), at])
        fetch(sides[f].at[1], prev_ext.at[:, pl.ds(HALO, block_x), at])
        for e in range(2):
            for ext, packed, reach in (
                (now_ext, corners_now, REACH_NOW),
                (prev_ext, corners_prev, REACH_PREV),
            ):
                place_corner(ext, packed[f].at[e], reach, e, f)

    x_first = lax.axis_index("gx") * block_x - HALO
    y_first = lax.axis_index("gy") * block_y - own
    shape = (rows, depth)
    y_in, y_depth = depth_in(lax.broadcasted_iota(jnp.int32, shape, 0) + y_first, total_y, block_x)
    y_part = y_depth * y_depth

    def weigh(x, _):
        x_in, x_depth = depth_in(jnp.full(shape, x + x_first, jnp.int32), total_x, block_x)
        twice[x] = jnp.where(
            x_in & y_in, 2.0 / (1.0 + damp_peak * (x_depth * x_depth + y_part)), 0.0
        )
        return 0

    lax.fori_loop(2, planes - 2, weigh, 0)
    for copy in copies:
        copy.wait()


def call_with_groups(kernel, sizes, counts):
    def called(*refs):
        groups = []
        for count in counts:
            groups.append(refs[0] if count is None else refs[:count])
            refs = refs[1 if count is None else count:]
        kernel(sizes, *groups, *refs)

    return called


def assemble(sizes, now, prev, now_x, prev_x, sides, corners):
    block_x, block_y, _, _, ny = sizes
    shots, _, _, depth = now.shape
    planes = block_x + 2 * HALO
    rows = block_y + (HALO if ny == 2 else 2 * HALO) + 2 * PAD
    count = len(sides)
    parts = [in_hbm(now), in_hbm(prev), *now_x, *prev_x, *sides, *corners[0], *corners[1]]
    return pl.pallas_call(
        call_with_groups(assemble_kernel, sizes, (None, None, 2, 2, count, count, count)),
        out_shape=pltpu.VMEM((2 * shots + 2, planes, rows, depth), jnp.float32),
        in_specs=[ANY] * len(parts),
        out_specs=VMEM,
        scratch_shapes=[pltpu.SemaphoreType.DMA((64,))],
        compiler_params=pltpu.CompilerParams(vmem_limit_bytes=SMALL),
        name="assemble_fields",
    )(*parts)


def window_kernel(
    sizes,
    sources,
    amplitudes,
    local_list,
    _,
    speed,
    speed_x,
    speed_y,
    speed_xy,
    out_now,
    out_prev,
    partial,
    ext_all,
    samples,
    sems,
    out_sems,
):
    block_x, block_y, total_x, total_y, ny = sizes
    shots = (ext_all.shape[0] - 2) // 2
    now_ext, prev_ext = ext_all.at[pl.ds(0, shots)], ext_all.at[pl.ds(shots, shots)]
    near, twice = ext_all.at[2 * shots], ext_all.at[2 * shots + 1]
    planes, rows = ext_all.shape[1:3]
    own, odd_y, high_x, x_at, y_at, near_y = layout(sizes)
    own_rows = pl.ds(own, block_y)
    x_first = lax.axis_index("gx") * block_x - HALO
    y_first = lax.axis_index("gy") * block_y - own
    copies = []

    def fetch(src, dst):
        copy = pltpu.make_async_copy(src, dst, sems.at[len(copies)])
        copy.start()
        copies.append(copy)

    fetch(speed, near.at[pl.ds(HALO, block_x), own_rows])
    for e in range(2):
        fetch(speed_x[e], near.at[pl.ds(x_at[e], block_x), own_rows])
    for f in range(len(speed_y)):
        at = pl.ds(y_at[f], HALO)
        fetch(speed_y[f], near.at[pl.ds(HALO, block_x), at])
        for e in range(2):
            fetch(speed_xy[2 * f + e], near.at[pl.ds(x_at[e], block_x), at])
    for k in range(shots * STEPS):
        samples[k] = jnp.zeros(samples.shape[1:], jnp.float32)
    for copy in copies:
        copy.wait()

    def prepare(x, _):
        at = pl.ds(PAD, rows - 2 * PAD)
        v = near[x, at]
        near[x, at] = (0.5 * near_weight) * twice[x, at] * (v * v)
        return 0

    lax.fori_loop(2, planes - 2, prepare, 0, unroll=2)

    depth = now_ext.shape[3]
    gap = lax.broadcasted_iota(jnp.int32, (depth, depth), 0) - lax.broadcasted_iota(jnp.int32, (depth, depth), 1)
    gap = jnp.abs(gap)
    band = jnp.where(gap == 0, centre_part, jnp.where(gap == 1, 1.0, jnp.where(gap == 2, far_part, 0.0)))
    band = band.astype(jnp.bfloat16)
    band = jnp.concatenate([band, band], axis=0)
    lane_row = lax.broadcasted_iota(jnp.int32, (1, depth), 1)

    cur, old = now_ext, prev_ext
    for step in range(1, STEPS + 1):
        reach = 2 * (STEPS - step)
        side = -(-reach // 8)
        if ny == 2:
            first = pl.multiple_of(own - 8 * side * odd_y, 8)
            tiles = block_y // 8 + side
        else:
            first = pl.multiple_of(own - 8 * side, 8)
            tiles = block_y // 8 + 2 * side

        size = 8 * tiles

        def some(g, _, at_x, size_x, first, tiles, cur=cur, old=old):
            x = at_x + size_x * g
            for j0 in range(0, tiles, 3):
                sub = min(3, tiles - j0)
                size = 8 * sub
                start = pl.multiple_of(first + 8 * j0, 8)
                along = []
                for s in range(shots):
                    c = cur[s, pl.ds(x, size_x), pl.ds(start, size)].reshape(size_x * size, depth)
                    head = c.astype(jnp.bfloat16)
                    rest = (c - head.astype(jnp.float32)).astype(jnp.bfloat16)
                    parts = jnp.concatenate([head, rest], axis=1)
                    out = jnp.dot(parts, band, preferred_element_type=jnp.float32)
                    along.append(out.reshape(size_x, size, depth))
                for j in range(sub):
                    base = start + 8 * j
                    at = pl.ds(pl.multiple_of(base, 8), 8)
                    n = [near[x + i, at] for i in range(size_x)]
                    a = [twice[x + i, at] for i in range(size_x)]
                    for s in range(shots):
                        c = [cur[s, x + i - 2, at] for i in range(size_x + 4)]
                        out = []
                        for i in range(size_x):
                            m = c[i + 2]
                            close = (c[i + 1] + c[i + 3]) + (cur[s, x + i, pl.ds(base - 1, 8)] + cur[s, x + i, pl.ds(base + 1, 8)])
                            wide = (c[i] + c[i + 4]) + (cur[s, x + i, pl.ds(base - 2, 8)] + cur[s, x + i, pl.ds(base + 2, 8)])
                            p = old[s, x + i, at]
                            lap = along[s][i, 8 * j : 8 * j + 8] + close + far_part * wide
                            out.append(p + a[i] * (m - p) + n[i] * lap)
                        for i in range(size_x):
                            old[s, x + i, at] = out[i]
            return 0

        def sweep(at_x, count, first, tiles):
            size_x = max(n for n in range(1, WIDEST + 1) if count % n == 0)
            part = functools.partial(some, at_x=at_x, size_x=size_x, first=first, tiles=tiles)
            lax.fori_loop(0, count // size_x, part, 0)

        edge = 8 if side == 2 else 0
        if edge:
            near_first = pl.multiple_of(own - 8 * (odd_y if ny == 2 else 1), 8)
            near_tiles = tiles - (1 if ny == 2 else 2)
            sweep(2 * step, edge, near_first, near_tiles)
            sweep(planes - 2 * step - edge, edge, near_first, near_tiles)
        sweep(2 * step + edge, planes - 4 * step - 2 * edge, first, tiles)

        for s in range(shots):
            sx = sources[s, 0] - x_first
            sy = sources[s, 1] - y_first
            sz = sources[s, 2]
            amplitude = amplitudes[s, step - 1]
            inside = (
                (sx >= 2 * step)
                & (sx < planes - 2 * step)
                & (sy >= first)
                & (sy < first + 8 * tiles)
            )

            @pl.when(inside)
            def _(old=old, s=s, sx=sx, sy=sy, sz=sz, amplitude=amplitude):
                at = pl.ds(sy, 1)
                old[s, sx, at] += jnp.where(lane_row == sz, (0.5 * amplitude) * twice[sx, at], 0.0)

        cur, old = old, cur

        def take(g, _, cur=cur, step=step):
            found = []
            for i in range(BATCH):
                at = 1 + 3 * (BATCH * g + i)
                cell, z = local_list[at + 1], local_list[at + 2]
                x = HALO + cell // block_y
                y = own + cell % block_y
                for s in range(shots):
                    found.append(jnp.where(lane_row == z, cur[s, x, pl.ds(y, 1)], 0.0))
            for i in range(BATCH):
                r = local_list[1 + 3 * (BATCH * g + i)]
                for s in range(shots):
                    samples[s * STEPS + step - 1, pl.ds(r, 1)] = found[i * shots + s]
            return 0

        lax.fori_loop(0, (local_list[0] + BATCH - 1) // BATCH, take, 0)
        if step >= STEPS - 1:
            out = out_prev if step == STEPS - 1 else out_now
            copy = pltpu.make_async_copy(
                cur.at[:, pl.ds(HALO, block_x), own_rows],
                out,
                out_sems.at[step - STEPS + 1],
            )
            copy.start()
            if step == STEPS - 1:
                first_out = copy
            else:
                last_out = copy

    total = partial.shape[2]
    values = jnp.sum(samples[:, pl.ds(0, total)], axis=2)
    for copy_to in range(partial.shape[0]):
        partial[copy_to] = values
    first_out.wait()
    last_out.wait()


def window(sizes, sources, amplitudes, local_list, recs, ext_all, speed, speed_x, speed_y, speed_xy, copies):
    block_x, block_y, _, _, _ = sizes
    shots = (ext_all.shape[0] - 2) // 2
    depth = ext_all.shape[3]
    field = jax.ShapeDtypeStruct((shots, block_x, block_y, depth), jnp.float32)
    count = len(speed_y)
    parts = [speed, *speed_x, *speed_y, *speed_xy]
    return pl.pallas_call(
        call_with_groups(window_kernel, sizes, (None, None, None, None, None, 2, count, 2 * count)),
        out_shape=(
            field,
            field,
            jax.ShapeDtypeStruct((copies, shots * STEPS, recs), jnp.float32),
            pltpu.VMEM(ext_all.shape, jnp.float32),
        ),
        in_specs=[SMEM] * 3 + [VMEM] + [ANY] * len(parts),
        out_specs=(ANY, ANY, VMEM, VMEM),
        input_output_aliases={3: 3},
        scratch_shapes=[
            pltpu.VMEM((shots * STEPS, recs + 8, depth), jnp.float32),
            pltpu.SemaphoreType.DMA((16,)),
            pltpu.SemaphoreType.DMA((2,)),
        ],
        compiler_params=pltpu.CompilerParams(vmem_limit_bytes=16 * 2**20),
        name="wave_window",
    )(sources, amplitudes, local_list, ext_all, *parts)


def local(model_tiles, owner_map, offsets, field_now, field_prev, sources, wavelet, receivers):
    block_x, block_y, depth = model_tiles.shape
    nx, ny, groups = lax.axis_size("gx"), lax.axis_size("gy"), lax.axis_size("sy")
    row = lax.axis_index("gy")
    total_x, total_y = block_x * nx, block_y * ny
    now, prev = field_now[0], field_prev[0]
    x_perms = [pairs(nx, 0), pairs(nx, 1)]
    y_perms = [pairs(ny, f) for f in range(2 if ny > 2 else 1)]
    spread = lax.all_to_all(model_tiles, ("sy", "gx"), 0, 0, tiled=True)
    now_x = [lax.ppermute(now, "gx", perm) for perm in x_perms]
    packed = [pack_sides(f, now, prev) for f in range(len(y_perms))]
    shifts = [offsets] + [
        lax.ppermute(offsets, "sy", [(i, (i + turn) % groups) for i in range(groups)])
        for turn in range(1, groups)
    ]
    sides = [lax.ppermute(part, "gy", perm) for part, perm in zip(packed, y_perms)]
    spread, packed, shifts, later = lax.optimization_barrier((spread, packed, shifts, prev))
    other = lax.ppermute(spread, "core", [(0, 1), (1, 0)])
    prev_x = [lax.ppermute(later, "gx", perm) for perm in x_perms]
    local_list = list_receivers(block_x, block_y, receivers[0].T)

    def cut_corners(blocks, reach):
        return [pack_corners(f, reach, blocks) for f in range(len(y_perms))]

    def swap_corners(packed):
        return [lax.ppermute(part, "gy", perm) for part, perm in zip(packed, y_perms)]


    targets = groups * nx
    slice_shape = (targets, block_x // targets, block_y, depth)
    picked = pick(nx, shifts, owner_map, spread.reshape(slice_shape), other.reshape(slice_shape))
    picked, now_x, sides = lax.optimization_barrier((picked, now_x, sides))
    cut_now = cut_corners(now_x, REACH_NOW)
    corners_now = swap_corners(cut_now)
    speed = lax.all_to_all(picked.reshape(model_tiles.shape), ("sy", "gx"), 0, 0, tiled=True)
    speed, prev_x, corners_now, local_list = lax.optimization_barrier((speed, prev_x, corners_now, local_list))
    corners = (corners_now, swap_corners(cut_corners(prev_x, REACH_PREV)))
    speed_x = [lax.ppermute(speed, "gx", perm) for perm in x_perms]
    speed_y, speed_xy = [], []
    for f, perm in enumerate(y_perms):
        start = jnp.where(row % 2 == f, block_y - HALO, 0)
        part = lax.dynamic_slice_in_dim(speed, start, HALO, axis=1)
        speed_y.append(lax.ppermute(part, "gy", perm))
        speed_xy += [lax.ppermute(part, ("gx", "gy"), joint(x_perm, perm, ny)) for x_perm in x_perms]

    sizes = (block_x, block_y, total_x, total_y, ny)
    ext_all = assemble(sizes, now, prev, now_x, prev_x, sides, corners)
    out_now, out_prev, partial, _ = window(
        sizes, sources[0], wavelet[0], local_list, receivers.shape[1],
        ext_all, speed, speed_x, speed_y, speed_xy, nx * ny,
    )
    gathered = lax.all_to_all(partial, ("gx", "gy"), 0, 0, tiled=True)
    shots = now.shape[0]
    traces = jnp.sum(gathered, axis=0).reshape(shots, STEPS, -1).transpose(0, 2, 1)
    return (out_now[None], out_prev[None], traces[None])


def solution(mesh):
    shape = dict(zip(mesh.axis_names, mesh.devices.shape))
    cores = 2 if shape["shot"] % 2 == 0 else 1
    fine = Mesh(
        mesh.devices.reshape(shape["shot"] // cores, cores, shape["gx"], shape["gy"]),
        ("sy", "core", "gx", "gy"),
    )
    shot = ("sy", "core")
    field = P(shot, None, "gx", "gy", None)
    return jax.shard_map(
        local,
        mesh=fine,
        in_specs=(
            P(("sy", "core", "gx"), "gy", None),
            P(),
            P(shot),
            field,
            field,
            P(shot, None, None),
            P(shot, None, None),
            P(shot, None, None),
        ),
        out_specs=(field, field, P(shot, None, None, None)),
        check_vma=False,
    )
```
